256 devices in a mesh: wide: 32 (over y, x, core), narrow: 8 (over z).
Axes of the slice: x: 4, y: 4, z: 8, core: 2. Of those that a mesh axis runs over, the one named last changes fastest.
Arguments:
- points: float32 [262144, 128], P(('wide', 'narrow'))
- start_basis: float32 [32, 786432], P(None, ('wide', 'narrow')), may hold values from -6 to 6
Outputs:
- embedding: float32 [32, 262144], P(None, ('wide', 'narrow'))
The draws below stay inside these ranges and needn't reach their ends.
All inputs are finite; a program needn't handle non-finite values.
Results may differ from the reference program's by a relative error of at most 0.0003.
Values sent between devices are 32-bit elements; how exact they have to be, the bound alone decides.
A program may use at most 256 MiB of HBM per device.

```python
import jax
import jax.numpy as jnp
from jax import lax

DIM = 128
EMB = 32
NPTS = 1024
ITERS = 4
NS_STEPS = 16
PATCHES = 256
PATCH = 3072
NPOINTS = 262144
BASES = 786432


def draw_points(key, part):
    key = jax.random.fold_in(key, 11)
    scale_key, latent_key = jax.random.split(key, 2)
    col_scales = jnp.exp(jax.random.uniform(scale_key, (DIM,), jnp.float32, jnp.log(0.1), 0.0))
    latent = jax.random.normal(latent_key, (NPOINTS, DIM), jnp.float32)
    return latent * col_scales[None, :]


def block_levels(rng, shape, cuts, least, high):
    level = 1.0
    for axis_at, blocks in cuts:
        heights = jax.random.uniform(jax.random.fold_in(jax.random.fold_in(rng, 6), axis_at), (blocks,), jnp.float32, least / len(cuts), high / len(cuts))
        level = level * jnp.repeat(jnp.exp(heights), shape[axis_at] // blocks).reshape((-1,) + (1,) * (len(shape) - 1 - axis_at))
    return level


def scatter_about(rng, shape, deviation, limit, shards=(), kind=jnp.bfloat16):
    loudness = block_levels(rng, shape, shards, -0.22, 0.18) if shards else 1.0
    entries = jax.random.normal(rng, shape, jnp.float32) * deviation * loudness
    return jnp.minimum(jnp.maximum(entries, -limit), limit).astype(kind)


def setup_inputs(seed: int = 0) -> dict:
    keys = jax.random.split(jax.random.key(seed), 3)
    return {
        "points": draw_points(jax.random.fold_in(keys[2], 71), 0),
        "start_basis": scatter_about(keys[1], (EMB, BASES), 1.0, 6.0, ((1, 256),), jnp.float32),
    }


HIGHEST_PRECISION = lax.Precision.HIGHEST

def orthonormal(basis_in):
    covariance = jnp.dot(basis_in, basis_in.T, precision=HIGHEST_PRECISION)
    cholesky_factor = jnp.linalg.cholesky(covariance)
    return jax.scipy.linalg.solve_triangular(cholesky_factor, basis_in, lower=True)

def patch_embedding(patch_rows, basis_in):
    norms = lax.optimization_barrier(jnp.sum(patch_rows * patch_rows, axis=1))
    products = jnp.dot(patch_rows, patch_rows.T, precision=HIGHEST_PRECISION)
    kernel = jnp.exp(-(norms[:, None] + norms[None, :] - 2.0 * products) / (0.5 * DIM))
    kernel = kernel - lax.optimization_barrier(jnp.mean(kernel, axis=0, keepdims=True))
    kernel = kernel - lax.optimization_barrier(jnp.mean(kernel, axis=1, keepdims=True))
    operator = 0.5 * kernel
    basis_rows = orthonormal(basis_in)
    for iteration in range(ITERS):
        projected = jnp.dot(basis_rows, operator, precision=HIGHEST_PRECISION)
        if iteration + 1 < ITERS:
            basis_rows = orthonormal(projected)
    return projected / (lax.optimization_barrier(jnp.sum(projected * projected, axis=1, keepdims=True)) + 1e-06) ** 0.25

def procrustes(target, source):
    target_mean = lax.optimization_barrier(jnp.mean(target, axis=1, keepdims=True))
    source_mean = lax.optimization_barrier(jnp.mean(source, axis=1, keepdims=True))
    covariance = jnp.dot(source - source_mean, (target - target_mean).T, precision=HIGHEST_PRECISION)
    orthogonal = covariance / jnp.sqrt(jnp.sum(covariance * covariance) + 1e-06)
    for iteration in range(NS_STEPS):
        square = jnp.dot(orthogonal, orthogonal.T, precision=HIGHEST_PRECISION)
        orthogonal = 1.5 * orthogonal - 0.5 * jnp.dot(square, orthogonal, precision=HIGHEST_PRECISION)
    translation = target_mean[:, 0] - jnp.dot(orthogonal.T, source_mean[:, 0], precision=HIGHEST_PRECISION)
    return (orthogonal, translation)

def compose(earlier, later_map):
    rot_early, off_early = earlier
    rot_late, off_late = later_map
    rotation = jnp.einsum('...ij,...jk->...ik', rot_late, rot_early, precision=HIGHEST_PRECISION)
    offset = jnp.einsum('...ji,...j->...i', rot_early, off_late, precision=HIGHEST_PRECISION) + off_early
    return (rotation, offset)

def reference(points, start_basis):
    blocks = points.reshape(PATCHES, NPTS, DIM)
    basis_sets = start_basis.reshape(EMB, PATCHES, PATCH).transpose(1, 0, 2)

    def embed_patch(position):
        patch_rows = jnp.concatenate([blocks[(position - 1) % PATCHES], blocks[position], blocks[(position + 1) % PATCHES]], axis=0)
        return patch_embedding(patch_rows, basis_sets[position])
    positions = jnp.arange(PATCHES, dtype=jnp.int32)
    embedded = lax.map(embed_patch, positions)
    previous = jnp.roll(embedded, 1, axis=0)
    rotation, offset = jax.vmap(procrustes)(previous[:, :, NPTS:], embedded[:, :, :2 * NPTS])
    identity_rot = jnp.eye(EMB, dtype=rotation.dtype)

    def chain_step(running_map, transform):
        composite = compose(running_map, transform)
        return (composite, composite)
    start_map = (identity_rot, jnp.zeros((EMB,), rotation.dtype))
    _, (comp_rot, comp_off) = lax.scan(chain_step, start_map, (rotation, offset))
    aligned = jnp.einsum('nji,njp->nip', comp_rot, embedded, precision=HIGHEST_PRECISION) + comp_off[:, :, None]
    middle = aligned[:, :, NPTS:2 * NPTS]
    from_prev = jnp.roll(aligned[:, :, 2 * NPTS:], 1, axis=0)
    from_next = jnp.roll(aligned[:, :, :NPTS], -1, axis=0)
    has_prev = (positions >= 1).astype(middle.dtype)[:, None, None]
    has_next = (positions <= PATCHES - 2).astype(middle.dtype)[:, None, None]
    summed = middle + has_prev * from_prev + has_next * from_next
    result = summed / (1.0 + has_prev + has_next)
    return result.transpose(1, 0, 2).reshape(EMB, PATCHES * NPTS)
```

```python
import functools
import math

import jax
import jax.numpy as jnp
from jax import lax
from jax.experimental import pallas as pl
from jax.experimental.pallas import tpu as pltpu
from jax.sharding import PartitionSpec as P

DIM = 128
EMB = 32
BLOCK = 1024
PATCH = 3 * BLOCK
ITERS = 4
NS_STEPS = 16
CHUNKS = 4
CHUNK = BLOCK // CHUNKS
LOW = 8

F32 = jnp.float32
BF16 = jnp.bfloat16
NT = (((1,), (1,)), ((), ()))
HIGHEST = lax.Precision.HIGHEST
MESH = pl.DeviceIdType.MESH
SCALE = math.sqrt(2.0 * math.log2(math.e) / (0.5 * DIM))


def halves(value):
    high = value.astype(BF16)
    return high, (value - high.astype(F32)).astype(BF16)


def thirds(value):
    high = value.astype(BF16)
    rest = value - high.astype(F32)
    middle = rest.astype(BF16)
    return high, middle, (rest - middle.astype(F32)).astype(BF16)


def prepare(rows, left_ref, right_ref, at):
    count = rows.shape[0]
    scaled = rows * SCALE
    high, low = halves(scaled)
    norms = -0.5 * jnp.sum(scaled * scaled, axis=1, keepdims=True)
    n0, n1, n2 = (part.astype(F32) for part in thirds(norms))
    lane = lax.broadcasted_iota(jnp.int32, (count, DIM), 1)
    tail = jnp.where(
        lane == 0,
        n0,
        jnp.where(lane == 1, n1, jnp.where(lane == 2, n2, jnp.where(lane < 6, 1.0, 0.0))),
    )
    here = pl.ds(at, count)
    left_ref[here, 0:DIM] = high
    left_ref[here, DIM : 2 * DIM] = low
    left_ref[here, 2 * DIM : 3 * DIM] = high
    left_ref[here, 3 * DIM : 4 * DIM] = tail.astype(BF16)
    turned = scaled.T
    high, low = halves(turned)
    norms = -0.5 * jnp.sum(turned * turned, axis=0, keepdims=True)
    n0, n1, n2 = (part.astype(F32) for part in thirds(norms))
    row = lax.broadcasted_iota(jnp.int32, (DIM, count), 0)
    tail = jnp.where(
        row < 3,
        1.0,
        jnp.where(row == 3, n0, jnp.where(row == 4, n1, jnp.where(row == 5, n2, 0.0))),
    )
    right_ref[0:DIM, here] = high
    right_ref[DIM : 2 * DIM, here] = high
    right_ref[2 * DIM : 3 * DIM, here] = low
    right_ref[3 * DIM : 4 * DIM, here] = tail.astype(BF16)


def kernel_tile(left_ref, right_ref, high_ref, low_ref, rows, cols):
    power = jnp.dot(left_ref[rows, :], right_ref[:, cols], preferred_element_type=F32)
    high, low = halves(jnp.exp2(power))
    high_ref[rows, cols] = high
    low_ref[rows, cols] = low


def product_nt(a, b):
    rows = a.shape[0]
    pair_a = jnp.concatenate(halves(a), axis=0)
    pair_b = jnp.concatenate(halves(b), axis=0)
    full = lax.dot_general(pair_a, pair_b, NT, preferred_element_type=F32)
    return full[:rows, :rows] + (full[:rows, rows:] + full[rows:, :rows]) + full[rows:, rows:]


def inverse_factor(gram):
    n = gram.shape[0]
    lane = lax.broadcasted_iota(jnp.int32, (n, 128), 1)
    row = lax.broadcasted_iota(jnp.int32, (n, 128), 0)
    both = jnp.concatenate([gram, jnp.zeros((n, 128 - n), F32)], axis=1)
    both = jnp.where(lane == row + n, 1.0, both)
    for k in range(n - 1):
        pivot = both[k : k + 1, :] / both[k : k + 1, k : k + 1]
        both = jnp.where(row > k, both - both[:, k : k + 1] * pivot, both)
    diagonal = jnp.sum(jnp.where(lane == row, both, 0.0), axis=1, keepdims=True)
    return both[:, n : 2 * n] / jnp.sqrt(diagonal)


def small_times_wide(small, wide):
    s0, s1, s2 = thirds(small)
    w0, w1, w2 = thirds(wide)
    return jnp.dot(
        jnp.concatenate([s0, s1, s0, s2, s1, s0], axis=1),
        jnp.concatenate([w0, w0, w1, w0, w1, w2], axis=0),
        preferred_element_type=F32,
    )


def chained(first, later):
    lane = lax.broadcasted_iota(jnp.int32, first.shape, 1)
    turned = jnp.dot(first[:, :EMB], later, precision=HIGHEST, preferred_element_type=F32)
    return turned + jnp.where(lane == EMB, first, 0.0)


def chain_of(maps):
    while len(maps) > 1:
        joined = [chained(maps[i], maps[i + 1]) for i in range(0, len(maps) - 1, 2)]
        maps = joined + maps[len(maps) - len(maps) % 2 :]
    return maps[0]


def kernel(
    wide_count,
    narrow_count,
    points_ref,
    start_ref,
    out_ref,
    own_ref,
    near_ref,
    left_ref,
    right_ref,
    high_ref,
    low_ref,
    basis_ref,
    image_ref,
    send_ref,
    got_ref,
    ring_ref,
    low_maps_ref,
    high_maps_ref,
    next_map_ref,
    x_send,
    x_recv,
    e_send,
    e_recv,
    m_send,
    m_recv,
    n_send,
    n_recv,
):
    wide = lax.axis_index("wide")
    narrow = lax.axis_index("narrow")
    total = wide_count * narrow_count
    me = wide * narrow_count + narrow
    after = lax.rem(me + 1, total)
    before = lax.rem(me + total - 1, total)
    after_id = (lax.div(after, narrow_count), lax.rem(after, narrow_count))
    before_id = (lax.div(before, narrow_count), lax.rem(before, narrow_count))
    upper = lax.div(wide, LOW)
    lower = lax.rem(wide, LOW)
    uppers = wide_count // LOW

    def along_narrow(step):
        return (wide, lax.rem(narrow + step, narrow_count))

    def along_lower(step):
        return (upper * LOW + lax.rem(lower + step, LOW), narrow)

    def along_upper(step):
        return (lax.rem(upper + step, uppers) * LOW + lower, narrow)

    levels = (
        (along_narrow, narrow_count, narrow, ring_ref),
        (along_lower, LOW, lower, low_maps_ref),
        (along_upper, uppers, upper, high_maps_ref),
    )
    barrier = pltpu.get_barrier_semaphore()
    greeted = 0
    for peer in (after_id, before_id):
        pl.semaphore_signal(barrier, inc=1, device_id=peer, device_id_type=MESH)
        greeted += 1
    for peer_at, count, _, _ in levels:
        for step in range(1, count):
            pl.semaphore_signal(barrier, inc=1, device_id=peer_at(step), device_id_type=MESH)
            greeted += 1
    pl.semaphore_wait(barrier, greeted)

    def remote(source, target, send, recv, peer):
        return pltpu.make_async_remote_copy(
            src_ref=source,
            dst_ref=target,
            send_sem=send,
            recv_sem=recv,
            device_id=peer,
            device_id_type=MESH,
        )

    point_copies = []
    for c in range(CHUNKS):
        rows = points_ref.at[pl.ds(c * CHUNK, CHUNK), :]
        for side, peer in ((0, after_id), (1, before_id)):
            copy = remote(
                rows, near_ref.at[c, side], x_send.at[c, side], x_recv.at[c, side], peer
            )
            copy.start()
            point_copies.append(copy)

    order = [(BLOCK + c * CHUNK, c * CHUNK) for c in range(CHUNKS)]
    for c in range(CHUNKS):
        order.append((c * CHUNK, BLOCK + 2 * c * CHUNK))
        order.append((2 * BLOCK + c * CHUNK, BLOCK + (2 * c + 1) * CHUNK))
    for theirs, mine in order:
        basis_ref[:, mine : mine + CHUNK] = start_ref[:, theirs : theirs + CHUNK]
    for c in range(CHUNKS):
        prepare(points_ref[c * CHUNK : (c + 1) * CHUNK, :], left_ref, right_ref, c * CHUNK)
    kernel_tile(left_ref, right_ref, high_ref, low_ref, slice(0, BLOCK), slice(0, BLOCK))
    for c in range(CHUNKS):
        known = BLOCK + 2 * c * CHUNK
        grown = known + 2 * CHUNK
        for side in (0, 1):
            point_copies[2 * c + side].wait_recv()
            prepare(near_ref[c, side], left_ref, right_ref, known + side * CHUNK)
        kernel_tile(left_ref, right_ref, high_ref, low_ref, slice(0, grown), slice(known, grown))
        kernel_tile(left_ref, right_ref, high_ref, low_ref, slice(known, grown), slice(0, known))

    @pl.loop(0, ITERS)
    def _(_):
        basis = basis_ref[...]
        factor = inverse_factor(product_nt(basis, basis))
        centred = basis - jnp.mean(basis, axis=1, keepdims=True)
        basis_high, basis_low = halves(centred)
        pair = jnp.concatenate([basis_high, basis_low], axis=0)
        for c in range(3):
            cols = slice(c * BLOCK, (c + 1) * BLOCK)
            by_high = jnp.dot(pair, high_ref[:, cols], preferred_element_type=F32)
            by_low = jnp.dot(basis_high, low_ref[:, cols], preferred_element_type=F32)
            image_ref[:, cols] = by_high[:EMB] + (by_high[EMB:] + by_low)
        image = image_ref[...]
        image = 0.5 * (image - jnp.mean(image, axis=1, keepdims=True))
        basis_ref[...] = small_times_wide(factor, image)

    image = basis_ref[...]
    size = jnp.sum(image * image, axis=1, keepdims=True) + 1e-06
    embedded = image / jnp.sqrt(jnp.sqrt(size))
    send_ref[0] = embedded[:, :BLOCK]
    for c in range(CHUNKS):
        at = BLOCK + 2 * c * CHUNK
        send_ref[2, :, c * CHUNK : (c + 1) * CHUNK] = embedded[:, at : at + CHUNK]
        send_ref[1, :, c * CHUNK : (c + 1) * CHUNK] = embedded[:, at + CHUNK : at + 2 * CHUNK]
    block_copies = []
    for part, peer in ((0, after_id), (1, after_id), (2, before_id)):
        copy = remote(send_ref.at[part], got_ref.at[part], e_send.at[part], e_recv.at[part], peer)
        copy.start()
        block_copies.append(copy)
    block_copies[0].wait_recv()
    block_copies[1].wait_recv()

    source = jnp.concatenate([send_ref[2], send_ref[0]], axis=1)
    target = jnp.concatenate([got_ref[0], got_ref[1]], axis=1)
    source_mean = jnp.mean(source, axis=1, keepdims=True)
    target_mean = jnp.mean(target, axis=1, keepdims=True)
    covariance = product_nt(target - target_mean, source - source_mean)
    turn = covariance / jnp.sqrt(jnp.sum(covariance * covariance) + 1e-06)

    def newton_schulz(_, turn):
        square = lax.dot_general(
            turn, turn, NT, precision=HIGHEST, preferred_element_type=F32
        )
        return 1.5 * turn - 0.5 * jnp.dot(
            square, turn, precision=HIGHEST, preferred_element_type=F32
        )

    turn = lax.fori_loop(0, NS_STEPS, newton_schulz, turn)
    lane = lax.broadcasted_iota(jnp.int32, (EMB, 128), 1)
    row = lax.broadcasted_iota(jnp.int32, (EMB, 128), 0)
    moved = jnp.dot(
        turn,
        jnp.where(lane == EMB, source_mean, 0.0),
        precision=HIGHEST,
        preferred_element_type=F32,
    )
    own_map = jnp.concatenate([turn, jnp.zeros((EMB, 128 - EMB), F32)], axis=1)
    own_map = own_map + (jnp.where(lane == EMB, target_mean, 0.0) - moved)
    unit = jnp.where(lane == row, 1.0, 0.0)

    own_ref[...] = own_map
    next_copy = remote(own_ref, next_map_ref, n_send, n_recv, before_id)
    next_copy.start()
    level_copies = []
    passed = own_map
    prefix = None
    slot = 0
    for level, (peer_at, count, place, maps_ref) in enumerate(levels):
        maps_ref[place] = passed
        for step in range(1, count):
            copy = remote(
                maps_ref.at[place],
                maps_ref.at[place],
                m_send.at[slot + step - 1],
                m_recv.at[slot + step - 1],
                peer_at(step),
            )
            copy.start()
            level_copies.append(copy)
        for step in range(1, count):
            origin = lax.rem(place + count - step, count)
            remote(
                maps_ref.at[origin],
                maps_ref.at[origin],
                m_send.at[slot + step - 1],
                m_recv.at[slot + step - 1],
                peer_at(step),
            ).wait_recv()
        slot += count - 1
        maps = [maps_ref[j] for j in range(count)]
        if level + 1 < len(levels):
            passed = chain_of(maps)
        masked = []
        for j in range(count - 1):
            earlier = jnp.where(j < place, 1.0, 0.0).astype(F32)
            masked.append(earlier * maps[j] + (1.0 - earlier) * unit)
        earlier_maps = chain_of(masked)
        prefix = earlier_maps if prefix is None else chained(earlier_maps, prefix)

    has_prev = jnp.where(me > 0, 1.0, 0.0).astype(F32)
    has_next = jnp.where(me < total - 1, 1.0, 0.0).astype(F32)
    composite = chained(prefix, own_map)
    next_copy.wait_recv()
    following = chained(composite, next_map_ref[...])
    share = 1.0 / (1.0 + has_prev + has_next)
    maps = (composite * share, prefix * (has_prev * share), following * (has_next * share))
    offset = (maps[0] + maps[1] + maps[2])[:, EMB : EMB + 1]
    block_copies[2].wait_recv()
    columns = jnp.concatenate([send_ref[0], got_ref[1], got_ref[2]], axis=0)
    columns_high, columns_low = halves(columns)
    joined = jnp.concatenate([m[:, :EMB] for m in maps], axis=1)
    joined_high, joined_low = halves(joined)
    out_ref[...] = (
        jnp.dot(
            jnp.concatenate([joined_high, joined_low, joined_high], axis=1),
            jnp.concatenate([columns_high, columns_high, columns_low], axis=0),
            preferred_element_type=F32,
        )
        + offset
    )
    for copy in point_copies + block_copies + level_copies + [next_copy]:
        copy.wait_send()


def shards(wide_count, narrow_count, points, start_basis):
    messages = (narrow_count - 1) + (LOW - 1) + (wide_count // LOW - 1)
    in_vmem = pl.BlockSpec(memory_space=pltpu.VMEM)
    return pl.pallas_call(
        functools.partial(kernel, wide_count, narrow_count),
        out_shape=jax.ShapeDtypeStruct((EMB, BLOCK), F32),
        in_specs=[in_vmem, in_vmem],
        out_specs=in_vmem,
        scratch_shapes=[
            pltpu.VMEM((EMB, 128), F32),
            pltpu.VMEM((CHUNKS, 2, CHUNK, DIM), F32),
            pltpu.VMEM((PATCH, 4 * DIM), BF16),
            pltpu.VMEM((4 * DIM, PATCH), BF16),
            pltpu.VMEM((PATCH, PATCH), BF16),
            pltpu.VMEM((PATCH, PATCH), BF16),
            pltpu.VMEM((EMB, PATCH), F32),
            pltpu.VMEM((EMB, PATCH), F32),
            pltpu.VMEM((3, EMB, BLOCK), F32),
            pltpu.VMEM((3, EMB, BLOCK), F32),
            pltpu.VMEM((narrow_count, EMB, 128), F32),
            pltpu.VMEM((LOW, EMB, 128), F32),
            pltpu.VMEM((wide_count // LOW, EMB, 128), F32),
            pltpu.VMEM((EMB, 128), F32),
            pltpu.SemaphoreType.DMA((CHUNKS, 2)),
            pltpu.SemaphoreType.DMA((CHUNKS, 2)),
            pltpu.SemaphoreType.DMA((3,)),
            pltpu.SemaphoreType.DMA((3,)),
            pltpu.SemaphoreType.DMA((messages,)),
            pltpu.SemaphoreType.DMA((messages,)),
            pltpu.SemaphoreType.DMA,
            pltpu.SemaphoreType.DMA,
        ],
        compiler_params=pltpu.CompilerParams(
            collective_id=0, has_side_effects=True, vmem_limit_bytes=61 * 1024 * 1024
        ),
    )(points, start_basis)


def solution(mesh):
    placed = (P(("wide", "narrow"), None), P(None, ("wide", "narrow")))
    return jax.shard_map(
        functools.partial(shards, mesh.shape["wide"], mesh.shape["narrow"]),
        mesh=mesh,
        in_specs=placed,
        out_specs=P(None, ("wide", "narrow")),
        check_vma=False,
    )
```

```python
import functools
import math

import jax
import jax.numpy as jnp
from jax import lax
from jax.experimental import pallas as pl
from jax.experimental.pallas import tpu as pltpu
from jax.sharding import PartitionSpec as P

DIM = 128
EMB = 32
BLOCK = 1024
PATCH = 3 * BLOCK
ITERS = 4
NS_STEPS = 16
CHUNKS = 4
CHUNK = BLOCK // CHUNKS
MAP = 64
LOW = 8

F32 = jnp.float32
BF16 = jnp.bfloat16
NT = (((1,), (1,)), ((), ()))
HIGHEST = lax.Precision.HIGHEST
MESH = pl.DeviceIdType.MESH
SCALE = math.sqrt(2.0 * math.log2(math.e) / (0.5 * DIM))


def halves(value):
    high = value.astype(BF16)
    return high, (value - high.astype(F32)).astype(BF16)


def thirds(value):
    high = value.astype(BF16)
    rest = value - high.astype(F32)
    middle = rest.astype(BF16)
    return high, middle, (rest - middle.astype(F32)).astype(BF16)


def prepare(rows, left_ref, right_ref, at):
    count = rows.shape[0]
    scaled = rows * SCALE
    high, low = halves(scaled)
    norms = -0.5 * jnp.sum(scaled * scaled, axis=1, keepdims=True)
    n0, n1, n2 = (part.astype(F32) for part in thirds(norms))
    lane = lax.broadcasted_iota(jnp.int32, (count, DIM), 1)
    tail = jnp.where(
        lane == 0,
        n0,
        jnp.where(lane == 1, n1, jnp.where(lane == 2, n2, jnp.where(lane < 6, 1.0, 0.0))),
    )
    here = pl.ds(at, count)
    left_ref[here, 0:DIM] = high
    left_ref[here, DIM : 2 * DIM] = low
    left_ref[here, 2 * DIM : 3 * DIM] = high
    left_ref[here, 3 * DIM : 4 * DIM] = tail.astype(BF16)
    turned = scaled.T
    high, low = halves(turned)
    norms = -0.5 * jnp.sum(turned * turned, axis=0, keepdims=True)
    n0, n1, n2 = (part.astype(F32) for part in thirds(norms))
    row = lax.broadcasted_iota(jnp.int32, (DIM, count), 0)
    tail = jnp.where(
        row < 3,
        1.0,
        jnp.where(row == 3, n0, jnp.where(row == 4, n1, jnp.where(row == 5, n2, 0.0))),
    )
    right_ref[0:DIM, here] = high
    right_ref[DIM : 2 * DIM, here] = high
    right_ref[2 * DIM : 3 * DIM, here] = low
    right_ref[3 * DIM : 4 * DIM, here] = tail.astype(BF16)


def kernel_tile(left_ref, right_ref, high_ref, low_ref, rows, cols):
    power = jnp.dot(left_ref[rows, :], right_ref[:, cols], preferred_element_type=F32)
    high, low = halves(jnp.exp2(power))
    high_ref[rows, cols] = high
    low_ref[rows, cols] = low


def product_nt(a, b):
    rows = a.shape[0]
    pair_a = jnp.concatenate(halves(a), axis=0)
    pair_b = jnp.concatenate(halves(b), axis=0)
    full = lax.dot_general(pair_a, pair_b, NT, preferred_element_type=F32)
    return full[:rows, :rows] + (full[:rows, rows:] + full[rows:, :rows]) + full[rows:, rows:]


def inverse_factor(gram):
    n = gram.shape[0]
    lane = lax.broadcasted_iota(jnp.int32, (n, 128), 1)
    row = lax.broadcasted_iota(jnp.int32, (n, 128), 0)
    both = jnp.concatenate([gram, jnp.zeros((n, 128 - n), F32)], axis=1)
    both = jnp.where(lane == row + n, 1.0, both)
    for k in range(n - 1):
        pivot = both[k : k + 1, :] / both[k : k + 1, k : k + 1]
        both = jnp.where(row > k, both - both[:, k : k + 1] * pivot, both)
    diagonal = jnp.sum(jnp.where(lane == row, both, 0.0), axis=1, keepdims=True)
    return both[:, n : 2 * n] / jnp.sqrt(diagonal)


def small_times_wide(small, wide):
    small_high, small_low = halves(small)
    wide_high, wide_low = halves(wide)
    return jnp.dot(
        jnp.concatenate([small_high, small_low, small_high], axis=1),
        jnp.concatenate([wide_high, wide_high, wide_low], axis=0),
        preferred_element_type=F32,
    )


def chained(first, later):
    lane = lax.broadcasted_iota(jnp.int32, first.shape, 1)
    first_high, first_low = halves(first[:, :EMB])
    later_high, later_low = halves(later)
    by_high = jnp.dot(
        jnp.concatenate([first_high, first_low], axis=0), later_high, preferred_element_type=F32
    )
    by_low = jnp.dot(first_high, later_low, preferred_element_type=F32)
    moved = by_high[:EMB] + (by_high[EMB:] + by_low)
    return moved + jnp.where(lane == EMB, first, 0.0)


def packed(value):
    half = EMB // 2
    return jnp.concatenate([value[:half], value[half:]], axis=1)


def unpacked(value):
    return jnp.concatenate([value[:, :MAP], value[:, MAP:]], axis=0)


def chain_of(maps):
    while len(maps) > 1:
        joined = [chained(maps[i], maps[i + 1]) for i in range(0, len(maps) - 1, 2)]
        maps = joined + maps[len(maps) - len(maps) % 2 :]
    return maps[0]


def kernel(
    wide_count,
    narrow_count,
    points_ref,
    start_ref,
    out_ref,
    own_ref,
    near_ref,
    left_ref,
    right_ref,
    high_ref,
    low_ref,
    basis_ref,
    image_ref,
    columns_ref,
    stats_ref,
    near_stats_ref,
    send_ref,
    got_ref,
    ring_ref,
    low_maps_ref,
    high_maps_ref,
    next_map_ref,
    x_send,
    x_recv,
    e_send,
    e_recv,
    s_send,
    s_recv,
    m_send,
    m_recv,
    n_send,
    n_recv,
):
    wide = lax.axis_index("wide")
    narrow = lax.axis_index("narrow")
    total = wide_count * narrow_count
    me = wide * narrow_count + narrow
    after = lax.rem(me + 1, total)
    before = lax.rem(me + total - 1, total)
    after_id = (lax.div(after, narrow_count), lax.rem(after, narrow_count))
    before_id = (lax.div(before, narrow_count), lax.rem(before, narrow_count))
    upper = lax.div(wide, LOW)
    lower = lax.rem(wide, LOW)
    uppers = wide_count // LOW

    def along_narrow(step):
        return (wide, lax.rem(narrow + step, narrow_count))

    def along_lower(step):
        return (upper * LOW + lax.rem(lower + step, LOW), narrow)

    def along_upper(step):
        return (lax.rem(upper + step, uppers) * LOW + lower, narrow)

    levels = (
        (along_narrow, narrow_count, narrow, ring_ref),
        (along_lower, LOW, lower, low_maps_ref),
        (along_upper, uppers, upper, high_maps_ref),
    )
    barrier = pltpu.get_barrier_semaphore()
    greeted = 0
    for peer in (after_id, before_id):
        pl.semaphore_signal(barrier, inc=1, device_id=peer, device_id_type=MESH)
        greeted += 1
    for peer_at, count, _, _ in levels:
        for step in range(1, count):
            pl.semaphore_signal(barrier, inc=1, device_id=peer_at(step), device_id_type=MESH)
            greeted += 1
    pl.semaphore_wait(barrier, greeted)

    def remote(source, target, send, recv, peer):
        return pltpu.make_async_remote_copy(
            src_ref=source,
            dst_ref=target,
            send_sem=send,
            recv_sem=recv,
            device_id=peer,
            device_id_type=MESH,
        )

    point_copies = []
    for c in range(CHUNKS):
        for side, peer in ((0, after_id), (1, before_id)):
            at = BLOCK - (c + 1) * CHUNK if side == 0 else c * CHUNK
            rows = points_ref.at[pl.ds(at, CHUNK), :]
            copy = remote(
                rows, near_ref.at[c, side], x_send.at[c, side], x_recv.at[c, side], peer
            )
            copy.start()
            point_copies.append(copy)

    basis_ref[...] = start_ref[...]
    for c in range(CHUNKS):
        at = BLOCK + c * CHUNK
        prepare(points_ref[c * CHUNK : (c + 1) * CHUNK, :], left_ref, right_ref, at)
    tile = functools.partial(kernel_tile, left_ref, right_ref, high_ref, low_ref)
    tile(slice(BLOCK, 2 * BLOCK), slice(BLOCK, 2 * BLOCK))
    for c in range(CHUNKS):
        first, last = BLOCK - c * CHUNK, 2 * BLOCK + c * CHUNK
        known, grown = slice(first, last), slice(first - CHUNK, last + CHUNK)
        sides = (slice(first - CHUNK, first), slice(last, last + CHUNK))
        for side in (0, 1):
            point_copies[2 * c + side].wait_recv()
            prepare(near_ref[c, side], left_ref, right_ref, sides[side].start)
        for side in (0, 1):
            tile(grown, sides[side])
            tile(sides[side], known)

    def factor_and_pair():
        basis = basis_ref[...]
        factor = 0.5 * inverse_factor(product_nt(basis, basis))
        high, low = halves(basis - jnp.mean(basis, axis=1, keepdims=True))
        return factor, jnp.concatenate([high, low], axis=0)

    def product(pair, part):
        cols = slice(part * BLOCK, (part + 1) * BLOCK)
        by_high = jnp.dot(pair, high_ref[:, cols], preferred_element_type=F32)
        by_low = jnp.dot(pair[:EMB], low_ref[:, cols], preferred_element_type=F32)
        return by_high[:EMB] + (by_high[EMB:] + by_low)

    @pl.loop(0, ITERS - 1)
    def _(_):
        factor, pair = factor_and_pair()
        for part in range(3):
            image_ref[:, part * BLOCK : (part + 1) * BLOCK] = product(pair, part)
        image = image_ref[...]
        image = image - jnp.mean(image, axis=1, keepdims=True)
        basis_ref[...] = small_times_wide(factor, image)

    factor, pair = factor_and_pair()
    block_copies = []
    for part, peer in ((1, after_id), (2, after_id), (0, before_id)):
        send_ref[part] = small_times_wide(factor, product(pair, part))
        copy = remote(send_ref.at[part], got_ref.at[part], e_send.at[part], e_recv.at[part], peer)
        copy.start()
        block_copies.append(copy)
    image = jnp.concatenate([send_ref[0], send_ref[1], send_ref[2]], axis=1)
    image_mean = jnp.mean(image, axis=1, keepdims=True)
    centred = image - image_mean
    size = jnp.sum(centred * centred, axis=1, keepdims=True) + 1e-06
    image_scale = 1.0 / jnp.sqrt(jnp.sqrt(size))
    lane = lax.broadcasted_iota(jnp.int32, (EMB, 128), 1)
    stats_ref[...] = jnp.where(lane == 0, image_mean, image_scale)
    for side, peer in ((0, after_id), (1, before_id)):
        copy = remote(
            stats_ref, near_stats_ref.at[side], s_send.at[side], s_recv.at[side], peer
        )
        copy.start()
        block_copies.append(copy)
    block_copies[0].wait_recv()
    block_copies[1].wait_recv()

    source = jnp.concatenate([send_ref[0], send_ref[1]], axis=1)
    target = jnp.concatenate([got_ref[1], got_ref[2]], axis=1)
    source_mean = jnp.mean(source, axis=1, keepdims=True)
    target_mean = jnp.mean(target, axis=1, keepdims=True)
    covariance = product_nt(target - target_mean, (source - source_mean) * image_scale)
    block_copies[3].wait_recv()
    prev_mean, prev_scale = near_stats_ref[0, :, 0:1], near_stats_ref[0, :, 1:2]
    source_mean = (source_mean - image_mean) * image_scale
    target_mean = (target_mean - prev_mean) * prev_scale
    covariance = covariance * prev_scale
    turn = covariance / jnp.sqrt(jnp.sum(covariance * covariance) + 1e-06)

    def newton_schulz(_, turn):
        square = lax.dot_general(
            turn, turn, NT, precision=HIGHEST, preferred_element_type=F32
        )
        return 1.5 * turn - 0.5 * jnp.dot(
            square, turn, precision=HIGHEST, preferred_element_type=F32
        )

    turn = lax.fori_loop(0, NS_STEPS, newton_schulz, turn)
    lane = lax.broadcasted_iota(jnp.int32, (EMB, MAP), 1)
    row = lax.broadcasted_iota(jnp.int32, (EMB, MAP), 0)
    moved = jnp.dot(
        turn,
        jnp.where(lane == EMB, source_mean, 0.0),
        precision=HIGHEST,
        preferred_element_type=F32,
    )
    own_map = jnp.concatenate([turn, jnp.zeros((EMB, MAP - EMB), F32)], axis=1)
    own_map = own_map + (jnp.where(lane == EMB, target_mean, 0.0) - moved)
    unit = jnp.where(lane == row, 1.0, 0.0)

    own_ref[...] = packed(own_map)
    next_copy = remote(own_ref, next_map_ref, n_send, n_recv, before_id)
    level_copies = []
    passed = own_map
    prefix = None
    slot = 0
    for level, (peer_at, count, place, maps_ref) in enumerate(levels):
        maps_ref[place] = packed(passed)
        for step in range(1, count):
            copy = remote(
                maps_ref.at[place],
                maps_ref.at[place],
                m_send.at[slot + step - 1],
                m_recv.at[slot + step - 1],
                peer_at(step),
            )
            copy.start()
            level_copies.append(copy)
        if level == 0:
            next_copy.start()
            block_copies[2].wait_recv()
            block_copies[4].wait_recv()
            next_mean, next_scale = near_stats_ref[1, :, 0:1], near_stats_ref[1, :, 1:2]
            columns = jnp.concatenate(
                [
                    (send_ref[1] - image_mean) * image_scale,
                    (got_ref[2] - prev_mean) * prev_scale,
                    (got_ref[0] - next_mean) * next_scale,
                ],
                axis=0,
            )
            columns_high, columns_low = halves(columns)
            columns_ref[...] = jnp.concatenate([columns_high, columns_high, columns_low], axis=0)
        for step in range(1, count):
            origin = lax.rem(place + count - step, count)
            remote(
                maps_ref.at[origin],
                maps_ref.at[origin],
                m_send.at[slot + step - 1],
                m_recv.at[slot + step - 1],
                peer_at(step),
            ).wait_recv()
        slot += count - 1
        maps = [unpacked(maps_ref[j]) for j in range(count)]
        if level + 1 < len(levels):
            passed = chain_of(maps)
        masked = []
        for j in range(count - 1):
            earlier = jnp.where(j < place, 1.0, 0.0).astype(F32)
            masked.append(earlier * maps[j] + (1.0 - earlier) * unit)
        earlier_maps = chain_of(masked)
        prefix = earlier_maps if prefix is None else chained(earlier_maps, prefix)

    has_prev = jnp.where(me > 0, 1.0, 0.0).astype(F32)
    has_next = jnp.where(me < total - 1, 1.0, 0.0).astype(F32)
    composite = chained(prefix, own_map)
    next_copy.wait_recv()
    following = chained(composite, unpacked(next_map_ref[...]))
    share = 1.0 / (1.0 + has_prev + has_next)
    maps = (composite * share, prefix * (has_prev * share), following * (has_next * share))
    offset = (maps[0] + maps[1] + maps[2])[:, EMB : EMB + 1]
    joined_high, joined_low = halves(jnp.concatenate([m[:, :EMB] for m in maps], axis=1))
    out_ref[...] = (
        jnp.dot(
            jnp.concatenate([joined_high, joined_low, joined_high], axis=1),
            columns_ref[...],
            preferred_element_type=F32,
        )
        + offset
    )
    for copy in point_copies + block_copies + level_copies + [next_copy]:
        copy.wait_send()


def shards(wide_count, narrow_count, points, start_basis):
    messages = (narrow_count - 1) + (LOW - 1) + (wide_count // LOW - 1)
    in_vmem = pl.BlockSpec(memory_space=pltpu.VMEM)
    return pl.pallas_call(
        functools.partial(kernel, wide_count, narrow_count),
        out_shape=jax.ShapeDtypeStruct((EMB, BLOCK), F32),
        in_specs=[in_vmem, in_vmem],
        out_specs=in_vmem,
        scratch_shapes=[
            pltpu.VMEM((EMB // 2, 2 * MAP), F32),
            pltpu.VMEM((CHUNKS, 2, CHUNK, DIM), F32),
            pltpu.VMEM((PATCH, 4 * DIM), BF16),
            pltpu.VMEM((4 * DIM, PATCH), BF16),
            pltpu.VMEM((PATCH, PATCH), BF16),
            pltpu.VMEM((PATCH, PATCH), BF16),
            pltpu.VMEM((EMB, PATCH), F32),
            pltpu.VMEM((EMB, PATCH), F32),
            pltpu.VMEM((9 * EMB, BLOCK), BF16),
            pltpu.VMEM((EMB, 128), F32),
            pltpu.VMEM((2, EMB, 128), F32),
            pltpu.VMEM((3, EMB, BLOCK), F32),
            pltpu.VMEM((3, EMB, BLOCK), F32),
            pltpu.VMEM((narrow_count, EMB // 2, 2 * MAP), F32),
            pltpu.VMEM((LOW, EMB // 2, 2 * MAP), F32),
            pltpu.VMEM((wide_count // LOW, EMB // 2, 2 * MAP), F32),
            pltpu.VMEM((EMB // 2, 2 * MAP), F32),
            pltpu.SemaphoreType.DMA((CHUNKS, 2)),
            pltpu.SemaphoreType.DMA((CHUNKS, 2)),
            pltpu.SemaphoreType.DMA((3,)),
            pltpu.SemaphoreType.DMA((3,)),
            pltpu.SemaphoreType.DMA((2,)),
            pltpu.SemaphoreType.DMA((2,)),
            pltpu.SemaphoreType.DMA((messages,)),
            pltpu.SemaphoreType.DMA((messages,)),
            pltpu.SemaphoreType.DMA,
            pltpu.SemaphoreType.DMA,
        ],
        compiler_params=pltpu.CompilerParams(
            collective_id=0, has_side_effects=True, vmem_limit_bytes=61 * 1024 * 1024
        ),
    )(points, start_basis)


def solution(mesh):
    placed = (P(("wide", "narrow"), None), P(None, ("wide", "narrow")))
    return jax.shard_map(
        functools.partial(shards, mesh.shape["wide"], mesh.shape["narrow"]),
        mesh=mesh,
        in_specs=placed,
        out_specs=P(None, ("wide", "narrow")),
        check_vma=False,
    )
```

```python
import functools
import math

import jax
import jax.numpy as jnp
from jax import lax
from jax.experimental import pallas as pl
from jax.experimental.pallas import tpu as pltpu
from jax.sharding import PartitionSpec as P

DIM = 128
EMB = 32
BLOCK = 1024
PATCH = 3 * BLOCK
ITERS = 4
NS_STEPS = 16
CHUNKS = 4
CHUNK = BLOCK // CHUNKS
MAP = 64
LOW = 8

F32 = jnp.float32
BF16 = jnp.bfloat16
NT = (((1,), (1,)), ((), ()))
HIGHEST = lax.Precision.HIGHEST
MESH = pl.DeviceIdType.MESH
SCALE = math.sqrt(2.0 * math.log2(math.e) / (0.5 * DIM))


def halves(value):
    high = value.astype(BF16)
    return high, (value - high.astype(F32)).astype(BF16)


def thirds(value):
    high = value.astype(BF16)
    rest = value - high.astype(F32)
    middle = rest.astype(BF16)
    return high, middle, (rest - middle.astype(F32)).astype(BF16)


def prepare(rows, left_ref, right_ref, at):
    count = rows.shape[0]
    scaled = rows * SCALE
    high, low = halves(scaled)
    norms = -0.5 * jnp.sum(scaled * scaled, axis=1, keepdims=True)
    n0, n1, n2 = (part.astype(F32) for part in thirds(norms))
    lane = lax.broadcasted_iota(jnp.int32, (count, DIM), 1)
    tail = jnp.where(
        lane == 0,
        n0,
        jnp.where(lane == 1, n1, jnp.where(lane == 2, n2, jnp.where(lane < 6, 1.0, 0.0))),
    )
    here = pl.ds(at, count)
    left_ref[here, 0:DIM] = high
    left_ref[here, DIM : 2 * DIM] = low
    left_ref[here, 2 * DIM : 3 * DIM] = high
    left_ref[here, 3 * DIM : 4 * DIM] = tail.astype(BF16)
    turned = scaled.T
    high, low = halves(turned)
    norms = -0.5 * jnp.sum(turned * turned, axis=0, keepdims=True)
    n0, n1, n2 = (part.astype(F32) for part in thirds(norms))
    row = lax.broadcasted_iota(jnp.int32, (DIM, count), 0)
    tail = jnp.where(
        row < 3,
        1.0,
        jnp.where(row == 3, n0, jnp.where(row == 4, n1, jnp.where(row == 5, n2, 0.0))),
    )
    right_ref[0:DIM, here] = high
    right_ref[DIM : 2 * DIM, here] = high
    right_ref[2 * DIM : 3 * DIM, here] = low
    right_ref[3 * DIM : 4 * DIM, here] = tail.astype(BF16)


def kernel_tile(left_ref, right_ref, high_ref, low_ref, rows, cols):
    power = jnp.dot(left_ref[rows, :], right_ref[:, cols], preferred_element_type=F32)
    high, low = halves(jnp.exp2(power))
    high_ref[rows, cols] = high
    low_ref[rows, cols] = low


def product_nt(a, b):
    rows = a.shape[0]
    pair_a = jnp.concatenate(halves(a), axis=0)
    pair_b = jnp.concatenate(halves(b), axis=0)
    full = lax.dot_general(pair_a, pair_b, NT, preferred_element_type=F32)
    return full[:rows, :rows] + (full[:rows, rows:] + full[rows:, :rows]) + full[rows:, rows:]


def inverse_factor(gram):
    n = gram.shape[0]
    lane = lax.broadcasted_iota(jnp.int32, (n, 128), 1)
    row = lax.broadcasted_iota(jnp.int32, (n, 128), 0)
    both = jnp.concatenate([gram, jnp.zeros((n, 128 - n), F32)], axis=1)
    both = jnp.where(lane == row + n, 1.0, both)
    for k in range(n - 1):
        pivot = both[k : k + 1, :] / both[k : k + 1, k : k + 1]
        both = jnp.where(row > k, both - both[:, k : k + 1] * pivot, both)
    diagonal = jnp.sum(jnp.where(lane == row, both, 0.0), axis=1, keepdims=True)
    return both[:, n : 2 * n] / jnp.sqrt(diagonal)


def small_times_wide(small, wide):
    small_high, small_low = halves(small)
    wide_high, wide_low = halves(wide)
    return jnp.dot(
        jnp.concatenate([small_high, small_low, small_high], axis=1),
        jnp.concatenate([wide_high, wide_high, wide_low], axis=0),
        preferred_element_type=F32,
    )


def chained(first, later):
    lane = lax.broadcasted_iota(jnp.int32, first.shape, 1)
    first_high, first_low = halves(first[:, :EMB])
    later_high, later_low = halves(later)
    by_high = jnp.dot(
        jnp.concatenate([first_high, first_low], axis=0), later_high, preferred_element_type=F32
    )
    by_low = jnp.dot(first_high, later_low, preferred_element_type=F32)
    moved = by_high[:EMB] + (by_high[EMB:] + by_low)
    return moved + jnp.where(lane == EMB, first, 0.0)


def packed(value):
    half = EMB // 2
    return jnp.concatenate([value[:half], value[half:]], axis=1)


def unpacked(value):
    return jnp.concatenate([value[:, :MAP], value[:, MAP:]], axis=0)


def chain_of(maps):
    while len(maps) > 1:
        joined = [chained(maps[i], maps[i + 1]) for i in range(0, len(maps) - 1, 2)]
        maps = joined + maps[len(maps) - len(maps) % 2 :]
    return maps[0]


def kernel(
    wide_count,
    narrow_count,
    points_ref,
    start_ref,
    out_ref,
    own_ref,
    near_ref,
    left_ref,
    right_ref,
    high_ref,
    low_ref,
    basis_ref,
    image_ref,
    columns_ref,
    stats_ref,
    near_stats_ref,
    send_ref,
    got_ref,
    ring_ref,
    low_maps_ref,
    high_maps_ref,
    next_map_ref,
    x_send,
    x_recv,
    e_send,
    e_recv,
    s_send,
    s_recv,
    m_send,
    m_recv,
    n_send,
    n_recv,
):
    wide = lax.axis_index("wide")
    narrow = lax.axis_index("narrow")
    total = wide_count * narrow_count
    me = wide * narrow_count + narrow
    after = lax.rem(me + 1, total)
    before = lax.rem(me + total - 1, total)
    after_id = (lax.div(after, narrow_count), lax.rem(after, narrow_count))
    before_id = (lax.div(before, narrow_count), lax.rem(before, narrow_count))
    upper = lax.div(wide, LOW)
    lower = lax.rem(wide, LOW)
    uppers = wide_count // LOW

    def along_narrow(step):
        return (wide, lax.rem(narrow + step, narrow_count))

    def along_lower(step):
        return (upper * LOW + lax.rem(lower + step, LOW), narrow)

    def along_upper(step):
        return (lax.rem(upper + step, uppers) * LOW + lower, narrow)

    levels = (
        (along_narrow, narrow_count, narrow, ring_ref),
        (along_lower, LOW, lower, low_maps_ref),
        (along_upper, uppers, upper, high_maps_ref),
    )
    barrier = pltpu.get_barrier_semaphore()
    greeted = 0
    for peer in (after_id, before_id):
        pl.semaphore_signal(barrier, inc=1, device_id=peer, device_id_type=MESH)
        greeted += 1
    for peer_at, count, _, _ in levels:
        for step in range(1, count):
            pl.semaphore_signal(barrier, inc=1, device_id=peer_at(step), device_id_type=MESH)
            greeted += 1
    pl.semaphore_wait(barrier, greeted)

    def remote(source, target, send, recv, peer):
        return pltpu.make_async_remote_copy(
            src_ref=source,
            dst_ref=target,
            send_sem=send,
            recv_sem=recv,
            device_id=peer,
            device_id_type=MESH,
        )

    point_copies = []
    for c in range(CHUNKS):
        for side, peer in ((0, after_id), (1, before_id)):
            at = BLOCK - (c + 1) * CHUNK if side == 0 else c * CHUNK
            rows = points_ref.at[pl.ds(at, CHUNK), :]
            copy = remote(
                rows, near_ref.at[c, side], x_send.at[c, side], x_recv.at[c, side], peer
            )
            copy.start()
            point_copies.append(copy)

    basis_ref[...] = start_ref[...]
    for c in range(CHUNKS):
        at = BLOCK + c * CHUNK
        prepare(points_ref[c * CHUNK : (c + 1) * CHUNK, :], left_ref, right_ref, at)
    tile = functools.partial(kernel_tile, left_ref, right_ref, high_ref, low_ref)
    tile(slice(BLOCK, 2 * BLOCK), slice(BLOCK, 2 * BLOCK))
    for c in range(CHUNKS):
        first, last = BLOCK - c * CHUNK, 2 * BLOCK + c * CHUNK
        known, grown = slice(first, last), slice(first - CHUNK, last + CHUNK)
        sides = (slice(first - CHUNK, first), slice(last, last + CHUNK))
        for side in (0, 1):
            point_copies[2 * c + side].wait_recv()
            prepare(near_ref[c, side], left_ref, right_ref, sides[side].start)
        for side in (0, 1):
            tile(grown, sides[side])
            tile(sides[side], known)

    def factor_and_pair():
        basis = basis_ref[...]
        factor = 0.5 * inverse_factor(product_nt(basis, basis))
        high, low = halves(basis - jnp.mean(basis, axis=1, keepdims=True))
        return factor, jnp.concatenate([high, low], axis=0)

    def product(pair, part):
        cols = slice(part * BLOCK, (part + 1) * BLOCK)
        by_high = jnp.dot(pair, high_ref[:, cols], preferred_element_type=F32)
        by_low = jnp.dot(pair[:EMB], low_ref[:, cols], preferred_element_type=F32)
        return by_high[:EMB] + (by_high[EMB:] + by_low)

    @pl.loop(0, ITERS - 1)
    def _(_):
        factor, pair = factor_and_pair()
        for part in range(3):
            image_ref[:, part * BLOCK : (part + 1) * BLOCK] = product(pair, part)
        image = image_ref[...]
        image = image - jnp.mean(image, axis=1, keepdims=True)
        basis_ref[...] = small_times_wide(factor, image)

    factor, pair = factor_and_pair()
    block_copies = []
    for part, peer in ((1, after_id), (2, after_id), (0, before_id)):
        send_ref[part] = product(pair, part)
        copy = remote(send_ref.at[part], got_ref.at[part], e_send.at[part], e_recv.at[part], peer)
        copy.start()
        block_copies.append(copy)
    raw = jnp.concatenate([send_ref[0], send_ref[1], send_ref[2]], axis=1)
    raw_mean = jnp.mean(raw, axis=1, keepdims=True)
    image = small_times_wide(factor, raw - raw_mean)
    image = image - jnp.mean(image, axis=1, keepdims=True)
    size = jnp.sum(image * image, axis=1, keepdims=True) + 1e-06
    scale = 1.0 / jnp.sqrt(jnp.sqrt(size))
    to_embedded = jnp.concatenate([factor * scale, jnp.zeros((EMB, MAP - EMB), F32)], axis=1)
    lane = lax.broadcasted_iota(jnp.int32, (EMB, MAP), 1)
    row = lax.broadcasted_iota(jnp.int32, (EMB, MAP), 0)
    stats_ref[...] = packed(jnp.where(lane == EMB, raw_mean, to_embedded))
    for side, peer in ((0, after_id), (1, before_id)):
        copy = remote(
            stats_ref, near_stats_ref.at[side], s_send.at[side], s_recv.at[side], peer
        )
        copy.start()
        block_copies.append(copy)
    image_ref[:, : 2 * BLOCK] = image[:, : 2 * BLOCK] * scale

    source = image_ref[:, : 2 * BLOCK]
    source_mean = jnp.mean(source, axis=1, keepdims=True)
    source = source - source_mean
    block_copies[0].wait_recv()
    target = got_ref[1]
    covariance = product_nt(target, source[:, :BLOCK])
    target_mean = jnp.sum(target, axis=1, keepdims=True)
    block_copies[1].wait_recv()
    target = got_ref[2]
    covariance = covariance + product_nt(target, source[:, BLOCK:])
    target_mean = (target_mean + jnp.sum(target, axis=1, keepdims=True)) / (2.0 * BLOCK)
    block_copies[3].wait_recv()
    prev_stats = unpacked(near_stats_ref[0])
    prev_mean = prev_stats[:, EMB : EMB + 1]
    covariance = jnp.concatenate([covariance, jnp.zeros((EMB, MAP - EMB), F32)], axis=1)
    covariance = jnp.dot(
        prev_stats[:, :EMB],
        jnp.where(lane == EMB, target_mean - prev_mean, covariance),
        precision=HIGHEST,
        preferred_element_type=F32,
    )
    target_mean = covariance[:, EMB : EMB + 1]
    covariance = covariance[:, :EMB]
    turn = covariance / jnp.sqrt(jnp.sum(covariance * covariance) + 1e-06)

    def newton_schulz(_, turn):
        square = lax.dot_general(
            turn, turn, NT, precision=HIGHEST, preferred_element_type=F32
        )
        return 1.5 * turn - 0.5 * jnp.dot(
            square, turn, precision=HIGHEST, preferred_element_type=F32
        )

    turn = lax.fori_loop(0, NS_STEPS, newton_schulz, turn)
    moved = jnp.dot(
        turn,
        jnp.where(lane == EMB, source_mean, 0.0),
        precision=HIGHEST,
        preferred_element_type=F32,
    )
    own_map = jnp.concatenate([turn, jnp.zeros((EMB, MAP - EMB), F32)], axis=1)
    own_map = own_map + (jnp.where(lane == EMB, target_mean, 0.0) - moved)
    unit = jnp.where(lane == row, 1.0, 0.0)
    has_prev = jnp.where(me > 0, 1.0, 0.0).astype(F32)
    has_next = jnp.where(me < total - 1, 1.0, 0.0).astype(F32)
    share = 1.0 / (1.0 + has_prev + has_next)

    def gather_start(level, value):
        peer_at, count, place, maps_ref = levels[level]
        maps_ref[place] = packed(value)
        copies = []
        for step in range(1, count):
            copy = remote(
                maps_ref.at[place],
                maps_ref.at[place],
                m_send.at[slots[level] + step - 1],
                m_recv.at[slots[level] + step - 1],
                peer_at(step),
            )
            copy.start()
            copies.append(copy)
        return copies

    def gather_end(level):
        peer_at, count, place, maps_ref = levels[level]
        for step in range(1, count):
            origin = lax.rem(place + count - step, count)
            remote(
                maps_ref.at[origin],
                maps_ref.at[origin],
                m_send.at[slots[level] + step - 1],
                m_recv.at[slots[level] + step - 1],
                peer_at(step),
            ).wait_recv()
        maps = [unpacked(maps_ref[j]) for j in range(count)]
        masked = []
        for j in range(count - 1):
            earlier = jnp.where(j < place, 1.0, 0.0).astype(F32)
            masked.append(earlier * maps[j] + (1.0 - earlier) * unit)
        return maps, masked

    slots = (0, narrow_count - 1, narrow_count + LOW - 2)
    own_ref[...] = packed(own_map)
    level_copies = gather_start(0, own_map)
    next_copy = remote(own_ref, next_map_ref, n_send, n_recv, before_id)
    next_copy.start()
    block_copies[2].wait_recv()
    block_copies[4].wait_recv()
    next_stats = unpacked(near_stats_ref[1])
    columns = jnp.concatenate(
        [
            image_ref[:, BLOCK : 2 * BLOCK],
            small_times_wide(prev_stats[:, :EMB], got_ref[2] - prev_mean),
            small_times_wide(next_stats[:, :EMB], got_ref[0] - next_stats[:, EMB : EMB + 1]),
        ],
        axis=0,
    )
    columns_high, columns_low = halves(columns)
    columns_ref[...] = jnp.concatenate([columns_high, columns_high, columns_low], axis=0)
    maps, masked = gather_end(0)
    level_copies += gather_start(1, chain_of(maps))
    prefix = chain_of(masked)
    next_copy.wait_recv()
    own_and_next = chained(own_map, unpacked(next_map_ref[...]))
    maps, masked = gather_end(1)
    level_copies += gather_start(2, chain_of(maps))
    prefix = chained(chain_of(masked), prefix)
    maps = (
        chained(prefix, own_map) * share,
        prefix * (has_prev * share),
        chained(prefix, own_and_next) * (has_next * share),
    )
    joined_high, joined_low = halves(jnp.concatenate([m[:, :EMB] for m in maps], axis=1))
    aligned = jnp.dot(
        jnp.concatenate([joined_high, joined_low, joined_high], axis=1),
        columns_ref[...],
        preferred_element_type=F32,
    )
    aligned = aligned + (maps[0] + maps[1] + maps[2])[:, EMB : EMB + 1]
    _, masked = gather_end(2)
    outer = chain_of(masked)
    out_ref[...] = small_times_wide(outer[:, :EMB], aligned) + outer[:, EMB : EMB + 1]
    for copy in point_copies + block_copies + level_copies + [next_copy]:
        copy.wait_send()


def shards(wide_count, narrow_count, points, start_basis):
    messages = (narrow_count - 1) + (LOW - 1) + (wide_count // LOW - 1)
    in_vmem = pl.BlockSpec(memory_space=pltpu.VMEM)
    return pl.pallas_call(
        functools.partial(kernel, wide_count, narrow_count),
        out_shape=jax.ShapeDtypeStruct((EMB, BLOCK), F32),
        in_specs=[in_vmem, in_vmem],
        out_specs=in_vmem,
        scratch_shapes=[
            pltpu.VMEM((EMB // 2, 2 * MAP), F32),
            pltpu.VMEM((CHUNKS, 2, CHUNK, DIM), F32),
            pltpu.VMEM((PATCH, 4 * DIM), BF16),
            pltpu.VMEM((4 * DIM, PATCH), BF16),
            pltpu.VMEM((PATCH, PATCH), BF16),
            pltpu.VMEM((PATCH, PATCH), BF16),
            pltpu.VMEM((EMB, PATCH), F32),
            pltpu.VMEM((EMB, PATCH), F32),
            pltpu.VMEM((9 * EMB, BLOCK), BF16),
            pltpu.VMEM((EMB // 2, 2 * MAP), F32),
            pltpu.VMEM((2, EMB // 2, 2 * MAP), F32),
            pltpu.VMEM((3, EMB, BLOCK), F32),
            pltpu.VMEM((3, EMB, BLOCK), F32),
            pltpu.VMEM((narrow_count, EMB // 2, 2 * MAP), F32),
            pltpu.VMEM((LOW, EMB // 2, 2 * MAP), F32),
            pltpu.VMEM((wide_count // LOW, EMB // 2, 2 * MAP), F32),
            pltpu.VMEM((EMB // 2, 2 * MAP), F32),
            pltpu.SemaphoreType.DMA((CHUNKS, 2)),
            pltpu.SemaphoreType.DMA((CHUNKS, 2)),
            pltpu.SemaphoreType.DMA((3,)),
            pltpu.SemaphoreType.DMA((3,)),
            pltpu.SemaphoreType.DMA((2,)),
            pltpu.SemaphoreType.DMA((2,)),
            pltpu.SemaphoreType.DMA((messages,)),
            pltpu.SemaphoreType.DMA((messages,)),
            pltpu.SemaphoreType.DMA,
            pltpu.SemaphoreType.DMA,
        ],
        compiler_params=pltpu.CompilerParams(
            collective_id=0, has_side_effects=True, vmem_limit_bytes=61 * 1024 * 1024
        ),
    )(points, start_basis)


def solution(mesh):
    placed = (P(("wide", "narrow"), None), P(None, ("wide", "narrow")))
    return jax.shard_map(
        functools.partial(shards, mesh.shape["wide"], mesh.shape["narrow"]),
        mesh=mesh,
        in_specs=placed,
        out_specs=P(None, ("wide", "narrow")),
        check_vma=False,
    )
```

```python
import functools
import math

import jax
import jax.numpy as jnp
from jax import lax
from jax.experimental import pallas as pl
from jax.experimental.pallas import tpu as pltpu
from jax.sharding import PartitionSpec as P

DIM = 128
EMB = 32
BLOCK = 1024
PATCH = 3 * BLOCK
ITERS = 4
NS_STEPS = 16
CHUNKS = (256, 256, 256, 128, 128)
MAP = 64
LOW = 8

F32 = jnp.float32
BF16 = jnp.bfloat16
F8 = jnp.float8_e4m3fn
LOW_SCALE = 65536.0
F8_MAX = 448.0
NT = (((1,), (1,)), ((), ()))
HIGHEST = lax.Precision.HIGHEST
MESH = pl.DeviceIdType.MESH
SCALE = math.sqrt(2.0 * math.log2(math.e) / (0.5 * DIM))


def halves(value):
    high = value.astype(BF16)
    return high, (value - high.astype(F32)).astype(BF16)


def thirds(value):
    high = value.astype(BF16)
    rest = value - high.astype(F32)
    middle = rest.astype(BF16)
    return high, middle, (rest - middle.astype(F32)).astype(BF16)


def prepare(rows, left_ref, right_ref, weight_ref, weights_ref, at):
    count = rows.shape[0]
    scaled = rows * SCALE
    high, low = halves(scaled)
    norms = -0.5 * jnp.sum(scaled * scaled, axis=1, keepdims=True)
    n0, n1, n2 = (part.astype(F32) for part in thirds(norms))
    lane = lax.broadcasted_iota(jnp.int32, (count, DIM), 1)
    tail = jnp.where(
        lane == 0,
        n0,
        jnp.where(lane == 1, n1, jnp.where(lane == 2, n2, jnp.where(lane < 6, 1.0, 0.0))),
    )
    here = pl.ds(at, count)
    left_ref[here, 0:DIM] = high
    left_ref[here, DIM : 2 * DIM] = low
    left_ref[here, 2 * DIM : 3 * DIM] = high
    left_ref[here, 3 * DIM : 4 * DIM] = tail.astype(BF16)
    weight_ref[here, :] = jnp.broadcast_to(jnp.exp2(norms), (count, 128))
    turned = scaled.T
    high, low = halves(turned)
    norms = -0.5 * jnp.sum(turned * turned, axis=0, keepdims=True)
    n0, n1, n2 = (part.astype(F32) for part in thirds(norms))
    row = lax.broadcasted_iota(jnp.int32, (DIM, count), 0)
    tail = jnp.where(
        row < 3,
        1.0,
        jnp.where(row == 3, n0, jnp.where(row == 4, n1, jnp.where(row == 5, n2, 0.0))),
    )
    right_ref[0:DIM, here] = high
    right_ref[DIM : 2 * DIM, here] = high
    right_ref[2 * DIM : 3 * DIM, here] = low
    right_ref[3 * DIM : 4 * DIM, here] = tail.astype(BF16)
    weights_ref[:, here] = jnp.exp2(norms)


def kernel_tile(left_ref, right_ref, weight_ref, weights_ref, high_ref, low_ref, rows, cols):
    power = jnp.dot(left_ref[rows, :], right_ref[:, cols], preferred_element_type=F32)
    repeats = (cols.stop - cols.start) // 128
    value = jnp.exp2(power) - jnp.tile(weight_ref[rows, :], (1, repeats)) * weights_ref[:, cols]
    high = value.astype(BF16)
    rest = (value - high.astype(F32)) * LOW_SCALE
    high_ref[rows, cols] = high
    low_ref[rows, cols] = jnp.minimum(jnp.maximum(rest, -F8_MAX), F8_MAX).astype(F8)


def product_nt(a, b):
    rows = a.shape[0]
    pair_a = jnp.concatenate(halves(a), axis=0)
    pair_b = jnp.concatenate(halves(b), axis=0)
    full = lax.dot_general(pair_a, pair_b, NT, preferred_element_type=F32)
    return full[:rows, :rows] + (full[:rows, rows:] + full[rows:, :rows]) + full[rows:, rows:]


def inverse_factor(gram):
    n = gram.shape[0]
    lane = lax.broadcasted_iota(jnp.int32, (n, 128), 1)
    row = lax.broadcasted_iota(jnp.int32, (n, 128), 0)
    both = jnp.concatenate([gram, jnp.zeros((n, 128 - n), F32)], axis=1)
    both = jnp.where(lane == row + n, 1.0, both)
    for k in range(n - 1):
        pivot = both[k : k + 1, :] / both[k : k + 1, k : k + 1]
        both = jnp.where(row > k, both - both[:, k : k + 1] * pivot, both)
    diagonal = jnp.sum(jnp.where(lane == row, both, 0.0), axis=1, keepdims=True)
    return both[:, n : 2 * n] / jnp.sqrt(diagonal)


def small_times_wide(small, wide):
    small_high, small_low = halves(small)
    wide_high, wide_low = halves(wide)
    return jnp.dot(
        jnp.concatenate([small_high, small_low, small_high], axis=1),
        jnp.concatenate([wide_high, wide_high, wide_low], axis=0),
        preferred_element_type=F32,
    )


def chained(first, later):
    lane = lax.broadcasted_iota(jnp.int32, first.shape, 1)
    first_high, first_low = halves(first[:, :EMB])
    later_high, later_low = halves(later)
    by_high = jnp.dot(
        jnp.concatenate([first_high, first_low], axis=0), later_high, preferred_element_type=F32
    )
    by_low = jnp.dot(first_high, later_low, preferred_element_type=F32)
    moved = by_high[:EMB] + (by_high[EMB:] + by_low)
    return moved + jnp.where(lane == EMB, first, 0.0)


def packed(value):
    half = EMB // 2
    return jnp.concatenate([value[:half], value[half:]], axis=1)


def unpacked(value):
    return jnp.concatenate([value[:, :MAP], value[:, MAP:]], axis=0)


def chain_of(maps):
    while len(maps) > 1:
        joined = [chained(maps[i], maps[i + 1]) for i in range(0, len(maps) - 1, 2)]
        maps = joined + maps[len(maps) - len(maps) % 2 :]
    return maps[0]


def kernel(
    wide_count,
    narrow_count,
    points_ref,
    start_ref,
    out_ref,
    own_ref,
    near_ref,
    points,
    left_ref,
    right_ref,
    weight_ref,
    weights_ref,
    high_ref,
    low_ref,
    basis_ref,
    image_ref,
    columns_ref,
    stats_ref,
    near_stats_ref,
    send_ref,
    got_ref,
    ring_ref,
    low_maps_ref,
    high_maps_ref,
    next_map_ref,
    load_sem,
    x_send,
    x_recv,
    e_send,
    e_recv,
    s_send,
    s_recv,
    m_send,
    m_recv,
    n_send,
    n_recv,
):
    wide = lax.axis_index("wide")
    narrow = lax.axis_index("narrow")
    total = wide_count * narrow_count
    me = wide * narrow_count + narrow
    after = lax.rem(me + 1, total)
    before = lax.rem(me + total - 1, total)
    after_id = (lax.div(after, narrow_count), lax.rem(after, narrow_count))
    before_id = (lax.div(before, narrow_count), lax.rem(before, narrow_count))
    upper = lax.div(wide, LOW)
    lower = lax.rem(wide, LOW)
    uppers = wide_count // LOW

    def along_narrow(step):
        return (wide, lax.rem(narrow + step, narrow_count))

    def along_lower(step):
        return (upper * LOW + lax.rem(lower + step, LOW), narrow)

    def along_upper(step):
        return (lax.rem(upper + step, uppers) * LOW + lower, narrow)

    levels = (
        (along_narrow, narrow_count, narrow, ring_ref),
        (along_lower, LOW, lower, low_maps_ref),
        (along_upper, uppers, upper, high_maps_ref),
    )
    loads = (
        pltpu.make_async_copy(points_ref, points, load_sem.at[0]),
        pltpu.make_async_copy(start_ref, basis_ref, load_sem.at[1]),
    )
    for copy in loads:
        copy.start()
    barrier = pltpu.get_barrier_semaphore()
    greeted = 0
    for peer in (after_id, before_id):
        pl.semaphore_signal(barrier, inc=1, device_id=peer, device_id_type=MESH)
        greeted += 1
    for peer_at, count, _, _ in levels:
        for step in range(1, count):
            pl.semaphore_signal(barrier, inc=1, device_id=peer_at(step), device_id_type=MESH)
            greeted += 1
    pl.semaphore_wait(barrier, greeted)

    def remote(source, target, send, recv, peer):
        return pltpu.make_async_remote_copy(
            src_ref=source,
            dst_ref=target,
            send_sem=send,
            recv_sem=recv,
            device_id=peer,
            device_id_type=MESH,
        )

    point_copies = []
    done = 0
    for c, size in enumerate(CHUNKS):
        for side, peer in ((0, after_id), (1, before_id)):
            rows = pl.ds(BLOCK - done - size if side == 0 else done, size)
            copy = remote(
                points_ref.at[rows, :],
                near_ref.at[side, rows, :],
                x_send.at[c, side],
                x_recv.at[c, side],
                peer,
            )
            copy.start()
            point_copies.append(copy)
        done += size

    for copy in loads:
        copy.wait()
    origin = jnp.mean(points[...], axis=0, keepdims=True)
    operands = (left_ref, right_ref, weight_ref, weights_ref)
    tile = functools.partial(kernel_tile, *operands, high_ref, low_ref)
    for at in range(0, BLOCK, 256):
        prepare(points[at : at + 256, :] - origin, *operands, BLOCK + at)
    tile(slice(BLOCK, 2 * BLOCK), slice(BLOCK, 2 * BLOCK))
    first, last = BLOCK, 2 * BLOCK
    for c, size in enumerate(CHUNKS):
        known, grown = slice(first, last), slice(first - size, last + size)
        sides = (slice(first - size, first), slice(last, last + size))
        for side in (0, 1):
            point_copies[2 * c + side].wait_recv()
            at = sides[side].start
            here = pl.ds(at - 2 * BLOCK * side, size)
            prepare(near_ref[side, here, :] - origin, *operands, at)
        for side in (0, 1):
            tile(grown, sides[side])
            tile(sides[side], known)
        first, last = grown.start, grown.stop

    def factor_and_pair():
        basis = basis_ref[...]
        factor = 0.5 * inverse_factor(product_nt(basis, basis))
        basis = basis - jnp.mean(basis, axis=1, keepdims=True)
        pair = jnp.concatenate(halves(basis), axis=0)
        weighted = jnp.sum(basis * weights_ref[...], axis=1, keepdims=True)
        top = jnp.maximum(jnp.max(jnp.abs(basis), axis=1, keepdims=True), 1e-30)
        small = basis * (256.0 / top)
        small_high = small.astype(F8)
        small_low = (small - small_high.astype(F32)).astype(F8)
        small_pair = jnp.concatenate([small_high, small_low], axis=0)
        return factor, (pair, small_pair, top / (256.0 * LOW_SCALE), weighted)

    def product(basis, part):
        pair, small_pair, unit, weighted = basis
        cols = slice(part * BLOCK, (part + 1) * BLOCK)
        by_high = jnp.dot(pair, high_ref[:, cols], preferred_element_type=F32)
        by_low = jnp.dot(small_pair, low_ref[:, cols], preferred_element_type=F32)
        by_low = (by_low[:EMB] + by_low[EMB:]) * unit + weighted * weights_ref[:, cols]
        return by_high[:EMB] + (by_high[EMB:] + by_low)

    @pl.loop(0, ITERS - 1)
    def _(_):
        factor, pair = factor_and_pair()
        for part in range(3):
            image_ref[:, part * BLOCK : (part + 1) * BLOCK] = product(pair, part)
        image = image_ref[...]
        image = image - jnp.mean(image, axis=1, keepdims=True)
        basis_ref[...] = small_times_wide(factor, image)

    factor, pair = factor_and_pair()
    block_copies = []
    for part, peer in ((1, after_id), (2, after_id), (0, before_id)):
        send_ref[part] = product(pair, part)
        copy = remote(send_ref.at[part], got_ref.at[part], e_send.at[part], e_recv.at[part], peer)
        copy.start()
        block_copies.append(copy)
    raw = jnp.concatenate([send_ref[0], send_ref[1], send_ref[2]], axis=1)
    raw_mean = jnp.mean(raw, axis=1, keepdims=True)
    image = small_times_wide(factor, raw - raw_mean)
    image = image - jnp.mean(image, axis=1, keepdims=True)
    size = jnp.sum(image * image, axis=1, keepdims=True) + 1e-06
    scale = 1.0 / jnp.sqrt(jnp.sqrt(size))
    to_embedded = jnp.concatenate([factor * scale, jnp.zeros((EMB, MAP - EMB), F32)], axis=1)
    lane = lax.broadcasted_iota(jnp.int32, (EMB, MAP), 1)
    row = lax.broadcasted_iota(jnp.int32, (EMB, MAP), 0)
    stats_ref[...] = packed(jnp.where(lane == EMB, raw_mean, to_embedded))
    for side, peer in ((0, after_id), (1, before_id)):
        copy = remote(
            stats_ref, near_stats_ref.at[side], s_send.at[side], s_recv.at[side], peer
        )
        copy.start()
        block_copies.append(copy)
    image_ref[:, : 2 * BLOCK] = image[:, : 2 * BLOCK] * scale

    source = image_ref[:, : 2 * BLOCK]
    source_mean = jnp.mean(source, axis=1, keepdims=True)
    source = source - source_mean
    block_copies[0].wait_recv()
    target = got_ref[1]
    covariance = product_nt(target, source[:, :BLOCK])
    target_mean = jnp.sum(target, axis=1, keepdims=True)
    block_copies[1].wait_recv()
    target = got_ref[2]
    covariance = covariance + product_nt(target, source[:, BLOCK:])
    target_mean = (target_mean + jnp.sum(target, axis=1, keepdims=True)) / (2.0 * BLOCK)
    block_copies[3].wait_recv()
    prev_stats = unpacked(near_stats_ref[0])
    prev_mean = prev_stats[:, EMB : EMB + 1]
    covariance = jnp.concatenate([covariance, jnp.zeros((EMB, MAP - EMB), F32)], axis=1)
    covariance = jnp.dot(
        prev_stats[:, :EMB],
        jnp.where(lane == EMB, target_mean - prev_mean, covariance),
        precision=HIGHEST,
        preferred_element_type=F32,
    )
    target_mean = covariance[:, EMB : EMB + 1]
    covariance = covariance[:, :EMB]
    turn = covariance / jnp.sqrt(jnp.sum(covariance * covariance) + 1e-06)

    def newton_schulz(_, turn):
        square = lax.dot_general(
            turn, turn, NT, precision=HIGHEST, preferred_element_type=F32
        )
        return 1.5 * turn - 0.5 * jnp.dot(
            square, turn, precision=HIGHEST, preferred_element_type=F32
        )

    turn = lax.fori_loop(0, NS_STEPS, newton_schulz, turn)
    moved = jnp.dot(
        turn,
        jnp.where(lane == EMB, source_mean, 0.0),
        precision=HIGHEST,
        preferred_element_type=F32,
    )
    own_map = jnp.concatenate([turn, jnp.zeros((EMB, MAP - EMB), F32)], axis=1)
    own_map = own_map + (jnp.where(lane == EMB, target_mean, 0.0) - moved)
    unit = jnp.where(lane == row, 1.0, 0.0)
    has_prev = jnp.where(me > 0, 1.0, 0.0).astype(F32)
    has_next = jnp.where(me < total - 1, 1.0, 0.0).astype(F32)
    share = 1.0 / (1.0 + has_prev + has_next)

    def gather_start(level, value):
        peer_at, count, place, maps_ref = levels[level]
        maps_ref[place] = packed(value)
        copies = []
        for step in range(1, count):
            copy = remote(
                maps_ref.at[place],
                maps_ref.at[place],
                m_send.at[slots[level] + step - 1],
                m_recv.at[slots[level] + step - 1],
                peer_at(step),
            )
            copy.start()
            copies.append(copy)
        return copies

    def gather_end(level):
        peer_at, count, place, maps_ref = levels[level]
        for step in range(1, count):
            origin = lax.rem(place + count - step, count)
            remote(
                maps_ref.at[origin],
                maps_ref.at[origin],
                m_send.at[slots[level] + step - 1],
                m_recv.at[slots[level] + step - 1],
                peer_at(step),
            ).wait_recv()
        maps = [unpacked(maps_ref[j]) for j in range(count)]
        masked = []
        for j in range(count - 1):
            earlier = jnp.where(j < place, 1.0, 0.0).astype(F32)
            masked.append(earlier * maps[j] + (1.0 - earlier) * unit)
        return maps, masked

    slots = (0, narrow_count - 1, narrow_count + LOW - 2)
    own_ref[...] = packed(own_map)
    level_copies = gather_start(0, own_map)
    next_copy = remote(own_ref, next_map_ref, n_send, n_recv, before_id)
    next_copy.start()
    block_copies[2].wait_recv()
    block_copies[4].wait_recv()
    next_stats = unpacked(near_stats_ref[1])
    columns = jnp.concatenate(
        [
            image_ref[:, BLOCK : 2 * BLOCK],
            small_times_wide(prev_stats[:, :EMB], got_ref[2] - prev_mean),
            small_times_wide(next_stats[:, :EMB], got_ref[0] - next_stats[:, EMB : EMB + 1]),
        ],
        axis=0,
    )
    columns_high, columns_low = halves(columns)
    columns_ref[...] = jnp.concatenate([columns_high, columns_high, columns_low], axis=0)
    maps, masked = gather_end(0)
    level_copies += gather_start(1, chain_of(maps))
    prefix = chain_of(masked)
    next_copy.wait_recv()
    own_and_next = chained(own_map, unpacked(next_map_ref[...]))
    maps, masked = gather_end(1)
    level_copies += gather_start(2, chain_of(maps))
    prefix = chained(chain_of(masked), prefix)
    maps = (
        chained(prefix, own_map) * share,
        prefix * (has_prev * share),
        chained(prefix, own_and_next) * (has_next * share),
    )
    joined_high, joined_low = halves(jnp.concatenate([m[:, :EMB] for m in maps], axis=1))
    aligned = jnp.dot(
        jnp.concatenate([joined_high, joined_low, joined_high], axis=1),
        columns_ref[...],
        preferred_element_type=F32,
    )
    aligned = aligned + (maps[0] + maps[1] + maps[2])[:, EMB : EMB + 1]
    _, masked = gather_end(2)
    outer = chain_of(masked)
    out_ref[...] = small_times_wide(outer[:, :EMB], aligned) + outer[:, EMB : EMB + 1]
    for copy in point_copies + block_copies + level_copies + [next_copy]:
        copy.wait_send()


def shards(wide_count, narrow_count, points, start_basis):
    messages = (narrow_count - 1) + (LOW - 1) + (wide_count // LOW - 1)
    in_vmem = pl.BlockSpec(memory_space=pltpu.VMEM)
    return pl.pallas_call(
        functools.partial(kernel, wide_count, narrow_count),
        out_shape=jax.ShapeDtypeStruct((EMB, BLOCK), F32),
        in_specs=[pl.BlockSpec(memory_space=pl.ANY)] * 2,
        out_specs=in_vmem,
        scratch_shapes=[
            pltpu.VMEM((EMB // 2, 2 * MAP), F32),
            pltpu.VMEM((2, BLOCK, DIM), F32),
            pltpu.VMEM((BLOCK, DIM), F32),
            pltpu.VMEM((PATCH, 4 * DIM), BF16),
            pltpu.VMEM((4 * DIM, PATCH), BF16),
            pltpu.VMEM((PATCH, 128), F32),
            pltpu.VMEM((1, PATCH), F32),
            pltpu.VMEM((PATCH, PATCH), BF16),
            pltpu.VMEM((PATCH, PATCH), F8),
            pltpu.VMEM((EMB, PATCH), F32),
            pltpu.VMEM((EMB, PATCH), F32),
            pltpu.VMEM((9 * EMB, BLOCK), BF16),
            pltpu.VMEM((EMB // 2, 2 * MAP), F32),
            pltpu.VMEM((2, EMB // 2, 2 * MAP), F32),
            pltpu.VMEM((3, EMB, BLOCK), F32),
            pltpu.VMEM((3, EMB, BLOCK), F32),
            pltpu.VMEM((narrow_count, EMB // 2, 2 * MAP), F32),
            pltpu.VMEM((LOW, EMB // 2, 2 * MAP), F32),
            pltpu.VMEM((wide_count // LOW, EMB // 2, 2 * MAP), F32),
            pltpu.VMEM((EMB // 2, 2 * MAP), F32),
            pltpu.SemaphoreType.DMA((2,)),
            pltpu.SemaphoreType.DMA((len(CHUNKS), 2)),
            pltpu.SemaphoreType.DMA((len(CHUNKS), 2)),
            pltpu.SemaphoreType.DMA((3,)),
            pltpu.SemaphoreType.DMA((3,)),
            pltpu.SemaphoreType.DMA((2,)),
            pltpu.SemaphoreType.DMA((2,)),
            pltpu.SemaphoreType.DMA((messages,)),
            pltpu.SemaphoreType.DMA((messages,)),
            pltpu.SemaphoreType.DMA,
            pltpu.SemaphoreType.DMA,
        ],
        compiler_params=pltpu.CompilerParams(
            collective_id=0, has_side_effects=True, vmem_limit_bytes=61 * 1024 * 1024
        ),
    )(points, start_basis)


def solution(mesh):
    placed = (P(("wide", "narrow"), None), P(None, ("wide", "narrow")))
    return jax.shard_map(
        functools.partial(shards, mesh.shape["wide"], mesh.shape["narrow"]),
        mesh=mesh,
        in_specs=placed,
        out_specs=P(None, ("wide", "narrow")),
        check_vma=False,
    )
```

```python
import functools
import math

import jax
import jax.numpy as jnp
from jax import lax
from jax.experimental import pallas as pl
from jax.experimental.pallas import tpu as pltpu
from jax.sharding import PartitionSpec as P

DIM = 128
EMB = 32
BLOCK = 1024
PATCH = 3 * BLOCK
ITERS = 4
NS_STEPS = 16
CHUNKS = (256, 256, 256, 256)
MAP = 64
LOW = 8

F32 = jnp.float32
BF16 = jnp.bfloat16
F8 = jnp.float8_e4m3fn
LOW_SCALE = 65536.0
F8_MAX = 448.0
NT = (((1,), (1,)), ((), ()))
HIGHEST = lax.Precision.HIGHEST
MESH = pl.DeviceIdType.MESH
SCALE = math.sqrt(2.0 * math.log2(math.e) / (0.5 * DIM))


def halves(value):
    high = value.astype(BF16)
    return high, (value - high.astype(F32)).astype(BF16)


def thirds(value):
    high = value.astype(BF16)
    rest = value - high.astype(F32)
    middle = rest.astype(BF16)
    return high, middle, (rest - middle.astype(F32)).astype(BF16)


def prepare(rows, left_ref, right_ref, weight_ref, weights_ref, at):
    count = rows.shape[0]
    scaled = rows * SCALE
    high, low = halves(scaled)
    norms = -0.5 * jnp.sum(scaled * scaled, axis=1, keepdims=True)
    n0, n1, n2 = (part.astype(F32) for part in thirds(norms))
    lane = lax.broadcasted_iota(jnp.int32, (count, DIM), 1)
    tail = jnp.where(
        lane == 0,
        n0,
        jnp.where(lane == 1, n1, jnp.where(lane == 2, n2, jnp.where(lane < 6, 1.0, 0.0))),
    )
    here = pl.ds(at, count)
    left_ref[here, 0:DIM] = high
    left_ref[here, DIM : 2 * DIM] = low
    left_ref[here, 2 * DIM : 3 * DIM] = high
    left_ref[here, 3 * DIM : 4 * DIM] = tail.astype(BF16)
    weight_ref[here, :] = jnp.broadcast_to(jnp.exp2(norms), (count, 128))
    turned = scaled.T
    high, low = halves(turned)
    norms = -0.5 * jnp.sum(turned * turned, axis=0, keepdims=True)
    n0, n1, n2 = (part.astype(F32) for part in thirds(norms))
    row = lax.broadcasted_iota(jnp.int32, (DIM, count), 0)
    tail = jnp.where(
        row < 3,
        1.0,
        jnp.where(row == 3, n0, jnp.where(row == 4, n1, jnp.where(row == 5, n2, 0.0))),
    )
    right_ref[0:DIM, here] = high
    right_ref[DIM : 2 * DIM, here] = high
    right_ref[2 * DIM : 3 * DIM, here] = low
    right_ref[3 * DIM : 4 * DIM, here] = tail.astype(BF16)
    weights_ref[:, here] = jnp.exp2(norms)


def kernel_tile(left_ref, right_ref, weight_ref, weights_ref, high_ref, low_ref, rows, cols):
    power = jnp.dot(left_ref[rows, :], right_ref[:, cols], preferred_element_type=F32)
    repeats = (cols.stop - cols.start) // 128
    value = jnp.exp2(power) - jnp.tile(weight_ref[rows, :], (1, repeats)) * weights_ref[:, cols]
    high = value.astype(BF16)
    rest = (value - high.astype(F32)) * LOW_SCALE
    high_ref[rows, cols] = high
    low_ref[rows, cols] = jnp.minimum(jnp.maximum(rest, -F8_MAX), F8_MAX).astype(F8)


def product_nt(a, b):
    rows = a.shape[0]
    pair_a = jnp.concatenate(halves(a), axis=0)
    pair_b = jnp.concatenate(halves(b), axis=0)
    full = lax.dot_general(pair_a, pair_b, NT, preferred_element_type=F32)
    return full[:rows, :rows] + (full[:rows, rows:] + full[rows:, :rows]) + full[rows:, rows:]


def elimination(gram):
    n = gram.shape[0]
    lane = lax.broadcasted_iota(jnp.int32, (n, 128), 1)
    row = lax.broadcasted_iota(jnp.int32, (n, 128), 0)
    both = jnp.concatenate([gram, jnp.zeros((n, 128 - n), F32)], axis=1)
    return jnp.where(lane == row + n, 1.0, both)


def eliminated(both, columns):
    row = lax.broadcasted_iota(jnp.int32, both.shape, 0)
    for k in columns:
        pivot = both[k : k + 1, :] / both[k : k + 1, k : k + 1]
        both = jnp.where(row > k, both - both[:, k : k + 1] * pivot, both)
    return both


def inverse_factor(both):
    n = both.shape[0]
    lane = lax.broadcasted_iota(jnp.int32, both.shape, 1)
    row = lax.broadcasted_iota(jnp.int32, both.shape, 0)
    diagonal = jnp.sum(jnp.where(lane == row, both, 0.0), axis=1, keepdims=True)
    return both[:, n : 2 * n] / jnp.sqrt(diagonal)


def small_times_wide(small, wide):
    small_high, small_low = halves(small)
    wide_high, wide_low = halves(wide)
    return jnp.dot(
        jnp.concatenate([small_high, small_low, small_high], axis=1),
        jnp.concatenate([wide_high, wide_high, wide_low], axis=0),
        preferred_element_type=F32,
    )


def chained(first, later):
    lane = lax.broadcasted_iota(jnp.int32, first.shape, 1)
    first_high, first_low = halves(first[:, :EMB])
    later_high, later_low = halves(later)
    by_high = jnp.dot(
        jnp.concatenate([first_high, first_low], axis=0), later_high, preferred_element_type=F32
    )
    by_low = jnp.dot(first_high, later_low, preferred_element_type=F32)
    moved = by_high[:EMB] + (by_high[EMB:] + by_low)
    return moved + jnp.where(lane == EMB, first, 0.0)


def packed(value):
    half = EMB // 2
    return jnp.concatenate([value[:half], value[half:]], axis=1)


def unpacked(value):
    return jnp.concatenate([value[:, :MAP], value[:, MAP:]], axis=0)


def chain_of(maps):
    while len(maps) > 1:
        joined = [chained(maps[i], maps[i + 1]) for i in range(0, len(maps) - 1, 2)]
        maps = joined + maps[len(maps) - len(maps) % 2 :]
    return maps[0]


def kernel(
    wide_count,
    narrow_count,
    points_ref,
    start_ref,
    out_ref,
    own_ref,
    near_ref,
    points,
    left_ref,
    right_ref,
    weight_ref,
    weights_ref,
    high_ref,
    low_ref,
    basis_ref,
    image_ref,
    columns_ref,
    stats_ref,
    near_stats_ref,
    send_ref,
    got_ref,
    ring_ref,
    low_maps_ref,
    high_maps_ref,
    next_map_ref,
    load_sem,
    x_send,
    x_recv,
    e_send,
    e_recv,
    s_send,
    s_recv,
    m_send,
    m_recv,
    n_send,
    n_recv,
):
    wide = lax.axis_index("wide")
    narrow = lax.axis_index("narrow")
    total = wide_count * narrow_count
    me = wide * narrow_count + narrow
    after = lax.rem(me + 1, total)
    before = lax.rem(me + total - 1, total)
    after_id = (lax.div(after, narrow_count), lax.rem(after, narrow_count))
    before_id = (lax.div(before, narrow_count), lax.rem(before, narrow_count))
    upper = lax.div(wide, LOW)
    lower = lax.rem(wide, LOW)
    uppers = wide_count // LOW

    def along_narrow(step):
        return (wide, lax.rem(narrow + step, narrow_count))

    def along_lower(step):
        return (upper * LOW + lax.rem(lower + step, LOW), narrow)

    def along_upper(step):
        return (lax.rem(upper + step, uppers) * LOW + lower, narrow)

    levels = (
        (along_narrow, narrow_count, narrow, ring_ref),
        (along_lower, LOW, lower, low_maps_ref),
        (along_upper, uppers, upper, high_maps_ref),
    )
    loads = (
        pltpu.make_async_copy(points_ref, points, load_sem.at[0]),
        pltpu.make_async_copy(start_ref, basis_ref, load_sem.at[1]),
    )
    for copy in loads:
        copy.start()
    barrier = pltpu.get_barrier_semaphore()
    greeted = 0
    for peer in (after_id, before_id):
        pl.semaphore_signal(barrier, inc=1, device_id=peer, device_id_type=MESH)
        greeted += 1
    for peer_at, count, _, _ in levels:
        for step in range(1, count):
            pl.semaphore_signal(barrier, inc=1, device_id=peer_at(step), device_id_type=MESH)
            greeted += 1
    pl.semaphore_wait(barrier, greeted)

    def remote(source, target, send, recv, peer):
        return pltpu.make_async_remote_copy(
            src_ref=source,
            dst_ref=target,
            send_sem=send,
            recv_sem=recv,
            device_id=peer,
            device_id_type=MESH,
        )

    def start_now(copies):
        @pl.when(me >= 0)
        def _():
            for copy in copies:
                copy.start()

    point_copies = []
    done = 0
    for c, size in enumerate(CHUNKS):
        for side, peer in ((0, after_id), (1, before_id)):
            rows = pl.ds(BLOCK - done - size if side == 0 else done, size)
            copy = remote(
                points_ref.at[rows, :],
                near_ref.at[side, rows, :],
                x_send.at[c, side],
                x_recv.at[c, side],
                peer,
            )
            copy.start()
            point_copies.append(copy)
        done += size

    for copy in loads:
        copy.wait()
    origin = jnp.mean(points[...], axis=0, keepdims=True)
    operands = (left_ref, right_ref, weight_ref, weights_ref)
    tile = functools.partial(kernel_tile, *operands, high_ref, low_ref)
    for at in range(0, BLOCK, 256):
        prepare(points[at : at + 256, :] - origin, *operands, BLOCK + at)
    tile(slice(BLOCK, 2 * BLOCK), slice(BLOCK, 2 * BLOCK))
    first, last = BLOCK, 2 * BLOCK
    for c, size in enumerate(CHUNKS):
        known, grown = slice(first, last), slice(first - size, last + size)
        sides = (slice(first - size, first), slice(last, last + size))
        for side in (0, 1):
            point_copies[2 * c + side].wait_recv()
            at = sides[side].start
            here = pl.ds(at - 2 * BLOCK * side, size)
            prepare(near_ref[side, here, :] - origin, *operands, at)
        for side in (0, 1):
            tile(grown, sides[side])
            tile(sides[side], known)
        first, last = grown.start, grown.stop

    def elimination_and_basis():
        basis = basis_ref[...]
        both = elimination(product_nt(basis, basis))
        basis = basis - jnp.mean(basis, axis=1, keepdims=True)
        pair = jnp.concatenate(halves(basis), axis=0)
        weighted = jnp.sum(basis * weights_ref[...], axis=1, keepdims=True)
        top = jnp.maximum(jnp.max(jnp.abs(basis), axis=1, keepdims=True), 1e-30)
        small = basis * (256.0 / top)
        small_high = small.astype(F8)
        small_low = (small - small_high.astype(F32)).astype(F8)
        small_pair = jnp.concatenate([small_high, small_low], axis=0)
        return both, (pair, small_pair, top / (256.0 * LOW_SCALE), weighted)

    def product(basis, part):
        pair, small_pair, unit, weighted = basis
        cols = slice(part * BLOCK, (part + 1) * BLOCK)
        by_high = jnp.dot(pair, high_ref[:, cols], preferred_element_type=F32)
        by_low = jnp.dot(small_pair, low_ref[:, cols], preferred_element_type=F32)
        by_low = (by_low[:EMB] + by_low[EMB:]) * unit + weighted * weights_ref[:, cols]
        return by_high[:EMB] + (by_high[EMB:] + by_low)

    @pl.loop(0, ITERS - 1)
    def _(_):
        both, basis = elimination_and_basis()
        factor = 0.5 * inverse_factor(eliminated(both, range(EMB - 1)))
        for part in range(3):
            image_ref[:, part * BLOCK : (part + 1) * BLOCK] = product(basis, part)
        image = image_ref[...]
        image = image - jnp.mean(image, axis=1, keepdims=True)
        basis_ref[...] = small_times_wide(factor, image)

    both, basis = elimination_and_basis()
    block_copies = []
    thirds_of_steps = (range(0, 11), range(11, 21), range(21, EMB - 1))
    for steps, part, peer in zip(thirds_of_steps, (1, 2, 0), (after_id, after_id, before_id)):
        both = eliminated(both, steps)
        send_ref[part] = product(basis, part)
        copy = remote(send_ref.at[part], got_ref.at[part], e_send.at[part], e_recv.at[part], peer)
        start_now([copy])
        block_copies.append(copy)
    factor = 0.5 * inverse_factor(both)
    raw = jnp.concatenate([send_ref[0], send_ref[1], send_ref[2]], axis=1)
    raw_mean = jnp.mean(raw, axis=1, keepdims=True)
    image = small_times_wide(factor, raw - raw_mean)
    image = image - jnp.mean(image, axis=1, keepdims=True)
    size = jnp.sum(image * image, axis=1, keepdims=True) + 1e-06
    scale = 1.0 / jnp.sqrt(jnp.sqrt(size))
    to_embedded = jnp.concatenate([factor * scale, jnp.zeros((EMB, MAP - EMB), F32)], axis=1)
    lane = lax.broadcasted_iota(jnp.int32, (EMB, MAP), 1)
    row = lax.broadcasted_iota(jnp.int32, (EMB, MAP), 0)
    stats_ref[...] = packed(jnp.where(lane == EMB, raw_mean, to_embedded))
    for side, peer in ((0, after_id), (1, before_id)):
        copy = remote(
            stats_ref, near_stats_ref.at[side], s_send.at[side], s_recv.at[side], peer
        )
        block_copies.append(copy)
    start_now(block_copies[3:])
    image_ref[:, : 2 * BLOCK] = image[:, : 2 * BLOCK] * scale

    source = image_ref[:, : 2 * BLOCK]
    source_mean = jnp.mean(source, axis=1, keepdims=True)
    source = source - source_mean
    block_copies[0].wait_recv()
    target = got_ref[1]
    covariance = product_nt(target, source[:, :BLOCK])
    target_mean = jnp.sum(target, axis=1, keepdims=True)
    block_copies[1].wait_recv()
    target = got_ref[2]
    covariance = covariance + product_nt(target, source[:, BLOCK:])
    target_mean = (target_mean + jnp.sum(target, axis=1, keepdims=True)) / (2.0 * BLOCK)
    block_copies[3].wait_recv()
    prev_stats = unpacked(near_stats_ref[0])
    prev_mean = prev_stats[:, EMB : EMB + 1]
    covariance = jnp.concatenate([covariance, jnp.zeros((EMB, MAP - EMB), F32)], axis=1)
    covariance = jnp.dot(
        prev_stats[:, :EMB],
        jnp.where(lane == EMB, target_mean - prev_mean, covariance),
        precision=HIGHEST,
        preferred_element_type=F32,
    )
    target_mean = covariance[:, EMB : EMB + 1]
    covariance = covariance[:, :EMB]
    turn = covariance / jnp.sqrt(jnp.sum(covariance * covariance) + 1e-06)

    def newton_schulz(_, turn):
        square = lax.dot_general(
            turn, turn, NT, precision=HIGHEST, preferred_element_type=F32
        )
        return 1.5 * turn - 0.5 * jnp.dot(
            square, turn, precision=HIGHEST, preferred_element_type=F32
        )

    turn = lax.fori_loop(0, NS_STEPS, newton_schulz, turn)
    moved = jnp.dot(
        turn,
        jnp.where(lane == EMB, source_mean, 0.0),
        precision=HIGHEST,
        preferred_element_type=F32,
    )
    own_map = jnp.concatenate([turn, jnp.zeros((EMB, MAP - EMB), F32)], axis=1)
    own_map = own_map + (jnp.where(lane == EMB, target_mean, 0.0) - moved)
    unit = jnp.where(lane == row, 1.0, 0.0)
    has_prev = jnp.where(me > 0, 1.0, 0.0).astype(F32)
    has_next = jnp.where(me < total - 1, 1.0, 0.0).astype(F32)
    share = 1.0 / (1.0 + has_prev + has_next)

    def gather_start(level, value):
        peer_at, count, place, maps_ref = levels[level]
        maps_ref[place] = packed(value)
        copies = []
        for step in range(1, count):
            copy = remote(
                maps_ref.at[place],
                maps_ref.at[place],
                m_send.at[slots[level] + step - 1],
                m_recv.at[slots[level] + step - 1],
                peer_at(step),
            )
            copies.append(copy)
        start_now(copies)
        return copies

    def gather_end(level):
        peer_at, count, place, maps_ref = levels[level]
        for step in range(1, count):
            origin = lax.rem(place + count - step, count)
            remote(
                maps_ref.at[origin],
                maps_ref.at[origin],
                m_send.at[slots[level] + step - 1],
                m_recv.at[slots[level] + step - 1],
                peer_at(step),
            ).wait_recv()
        maps = [unpacked(maps_ref[j]) for j in range(count)]
        masked = []
        for j in range(count - 1):
            earlier = jnp.where(j < place, 1.0, 0.0).astype(F32)
            masked.append(earlier * maps[j] + (1.0 - earlier) * unit)
        return maps, masked

    slots = (0, narrow_count - 1, narrow_count + LOW - 2)
    own_ref[...] = packed(own_map)
    level_copies = gather_start(0, own_map)
    next_copy = remote(own_ref, next_map_ref, n_send, n_recv, before_id)
    start_now([next_copy])
    block_copies[2].wait_recv()
    block_copies[4].wait_recv()
    next_stats = unpacked(near_stats_ref[1])
    columns = jnp.concatenate(
        [
            image_ref[:, BLOCK : 2 * BLOCK],
            small_times_wide(prev_stats[:, :EMB], got_ref[2] - prev_mean),
            small_times_wide(next_stats[:, :EMB], got_ref[0] - next_stats[:, EMB : EMB + 1]),
        ],
        axis=0,
    )
    columns_high, columns_low = halves(columns)
    columns_ref[...] = jnp.concatenate([columns_high, columns_high, columns_low], axis=0)
    maps, masked = gather_end(0)
    level_copies += gather_start(1, chain_of(maps))
    prefix = chain_of(masked)
    next_copy.wait_recv()
    own_and_next = chained(own_map, unpacked(next_map_ref[...]))
    maps, masked = gather_end(1)
    level_copies += gather_start(2, chain_of(maps))
    prefix = chained(chain_of(masked), prefix)
    maps = (
        chained(prefix, own_map) * share,
        prefix * (has_prev * share),
        chained(prefix, own_and_next) * (has_next * share),
    )
    joined_high, joined_low = halves(jnp.concatenate([m[:, :EMB] for m in maps], axis=1))
    aligned = jnp.dot(
        jnp.concatenate([joined_high, joined_low, joined_high], axis=1),
        columns_ref[...],
        preferred_element_type=F32,
    )
    aligned = aligned + (maps[0] + maps[1] + maps[2])[:, EMB : EMB + 1]
    _, masked = gather_end(2)
    outer = chain_of(masked)
    out_ref[...] = small_times_wide(outer[:, :EMB], aligned) + outer[:, EMB : EMB + 1]
    for copy in point_copies + block_copies + level_copies + [next_copy]:
        copy.wait_send()


def shards(wide_count, narrow_count, points, start_basis):
    messages = (narrow_count - 1) + (LOW - 1) + (wide_count // LOW - 1)
    in_vmem = pl.BlockSpec(memory_space=pltpu.VMEM)
    return pl.pallas_call(
        functools.partial(kernel, wide_count, narrow_count),
        out_shape=jax.ShapeDtypeStruct((EMB, BLOCK), F32),
        in_specs=[pl.BlockSpec(memory_space=pl.ANY)] * 2,
        out_specs=in_vmem,
        scratch_shapes=[
            pltpu.VMEM((EMB // 2, 2 * MAP), F32),
            pltpu.VMEM((2, BLOCK, DIM), F32),
            pltpu.VMEM((BLOCK, DIM), F32),
            pltpu.VMEM((PATCH, 4 * DIM), BF16),
            pltpu.VMEM((4 * DIM, PATCH), BF16),
            pltpu.VMEM((PATCH, 128), F32),
            pltpu.VMEM((1, PATCH), F32),
            pltpu.VMEM((PATCH, PATCH), BF16),
            pltpu.VMEM((PATCH, PATCH), F8),
            pltpu.VMEM((EMB, PATCH), F32),
            pltpu.VMEM((EMB, PATCH), F32),
            pltpu.VMEM((9 * EMB, BLOCK), BF16),
            pltpu.VMEM((EMB // 2, 2 * MAP), F32),
            pltpu.VMEM((2, EMB // 2, 2 * MAP), F32),
            pltpu.VMEM((3, EMB, BLOCK), F32),
            pltpu.VMEM((3, EMB, BLOCK), F32),
            pltpu.VMEM((narrow_count, EMB // 2, 2 * MAP), F32),
            pltpu.VMEM((LOW, EMB // 2, 2 * MAP), F32),
            pltpu.VMEM((wide_count // LOW, EMB // 2, 2 * MAP), F32),
            pltpu.VMEM((EMB // 2, 2 * MAP), F32),
            pltpu.SemaphoreType.DMA((2,)),
            pltpu.SemaphoreType.DMA((len(CHUNKS), 2)),
            pltpu.SemaphoreType.DMA((len(CHUNKS), 2)),
            pltpu.SemaphoreType.DMA((3,)),
            pltpu.SemaphoreType.DMA((3,)),
            pltpu.SemaphoreType.DMA((2,)),
            pltpu.SemaphoreType.DMA((2,)),
            pltpu.SemaphoreType.DMA((messages,)),
            pltpu.SemaphoreType.DMA((messages,)),
            pltpu.SemaphoreType.DMA,
            pltpu.SemaphoreType.DMA,
        ],
        compiler_params=pltpu.CompilerParams(
            collective_id=0, has_side_effects=True, vmem_limit_bytes=61 * 1024 * 1024
        ),
    )(points, start_basis)


def solution(mesh):
    placed = (P(("wide", "narrow"), None), P(None, ("wide", "narrow")))
    return jax.shard_map(
        functools.partial(shards, mesh.shape["wide"], mesh.shape["narrow"]),
        mesh=mesh,
        in_specs=placed,
        out_specs=P(None, ("wide", "narrow")),
        check_vma=False,
    )
```

```python
import functools
import math

import jax
import jax.numpy as jnp
from jax import lax
from jax.experimental import pallas as pl
from jax.experimental.pallas import tpu as pltpu
from jax.sharding import PartitionSpec as P

DIM = 128
EMB = 32
BLOCK = 1024
PATCH = 3 * BLOCK
ITERS = 4
NS_STEPS = 16
CHUNKS = (256, 256, 256, 256)
MAP = 64
LOW = 8

F32 = jnp.float32
BF16 = jnp.bfloat16
F8 = jnp.float8_e4m3fn
LOW_SCALE = 65536.0
F8_MAX = 448.0
NT = (((1,), (1,)), ((), ()))
HIGHEST = lax.Precision.HIGHEST
MESH = pl.DeviceIdType.MESH
SCALE = math.sqrt(2.0 * math.log2(math.e) / (0.5 * DIM))


def halves(value):
    high = value.astype(BF16)
    return high, (value - high.astype(F32)).astype(BF16)


def thirds(value):
    high = value.astype(BF16)
    rest = value - high.astype(F32)
    middle = rest.astype(BF16)
    return high, middle, (rest - middle.astype(F32)).astype(BF16)


def prepare(rows, left_ref, right_ref, weight_ref, weights_ref, at):
    count = rows.shape[0]
    scaled = rows * SCALE
    high, low = halves(scaled)
    norms = -0.5 * jnp.sum(scaled * scaled, axis=1, keepdims=True)
    n0, n1, n2 = (part.astype(F32) for part in thirds(norms))
    lane = lax.broadcasted_iota(jnp.int32, (count, DIM), 1)
    tail = jnp.where(
        lane == 0,
        n0,
        jnp.where(lane == 1, n1, jnp.where(lane == 2, n2, jnp.where(lane < 6, 1.0, 0.0))),
    )
    here = pl.ds(at, count)
    left_ref[here, 0:DIM] = high
    left_ref[here, DIM : 2 * DIM] = low
    left_ref[here, 2 * DIM : 3 * DIM] = high
    left_ref[here, 3 * DIM : 4 * DIM] = tail.astype(BF16)
    weight_ref[here, :] = jnp.broadcast_to(jnp.exp2(norms), (count, 128))
    turned = scaled.T
    high, low = halves(turned)
    norms = -0.5 * jnp.sum(turned * turned, axis=0, keepdims=True)
    n0, n1, n2 = (part.astype(F32) for part in thirds(norms))
    row = lax.broadcasted_iota(jnp.int32, (DIM, count), 0)
    tail = jnp.where(
        row < 3,
        1.0,
        jnp.where(row == 3, n0, jnp.where(row == 4, n1, jnp.where(row == 5, n2, 0.0))),
    )
    right_ref[0:DIM, here] = high
    right_ref[DIM : 2 * DIM, here] = high
    right_ref[2 * DIM : 3 * DIM, here] = low
    right_ref[3 * DIM : 4 * DIM, here] = tail.astype(BF16)
    weights_ref[:, here] = jnp.exp2(norms)


def kernel_tile(left_ref, right_ref, weight_ref, weights_ref, high_ref, low_ref, rows, cols):
    power = jnp.dot(left_ref[rows, :], right_ref[:, cols], preferred_element_type=F32)
    repeats = (cols.stop - cols.start) // 128
    value = jnp.exp2(power) - jnp.tile(weight_ref[rows, :], (1, repeats)) * weights_ref[:, cols]
    keep(value, high_ref, low_ref, rows, cols)
    return value


def keep(value, high_ref, low_ref, rows, cols):
    high = value.astype(BF16)
    rest = (value - high.astype(F32)) * LOW_SCALE
    high_ref[rows, cols] = high
    low_ref[rows, cols] = jnp.minimum(jnp.maximum(rest, -F8_MAX), F8_MAX).astype(F8)


def product_nt(a, b):
    rows = a.shape[0]
    pair_a = jnp.concatenate(halves(a), axis=0)
    pair_b = jnp.concatenate(halves(b), axis=0)
    full = lax.dot_general(pair_a, pair_b, NT, preferred_element_type=F32)
    return full[:rows, :rows] + (full[:rows, rows:] + full[rows:, :rows]) + full[rows:, rows:]


def elimination(gram):
    n = gram.shape[0]
    lane = lax.broadcasted_iota(jnp.int32, (n, 128), 1)
    row = lax.broadcasted_iota(jnp.int32, (n, 128), 0)
    both = jnp.concatenate([gram, jnp.zeros((n, 128 - n), F32)], axis=1)
    return jnp.where(lane == row + n, 1.0, both)


def eliminated(both, columns):
    row = lax.broadcasted_iota(jnp.int32, both.shape, 0)
    for k in columns:
        pivot = both[k : k + 1, :] / both[k : k + 1, k : k + 1]
        both = jnp.where(row > k, both - both[:, k : k + 1] * pivot, both)
    return both


def inverse_factor(both):
    n = both.shape[0]
    lane = lax.broadcasted_iota(jnp.int32, both.shape, 1)
    row = lax.broadcasted_iota(jnp.int32, both.shape, 0)
    diagonal = jnp.sum(jnp.where(lane == row, both, 0.0), axis=1, keepdims=True)
    return both[:, n : 2 * n] / jnp.sqrt(diagonal)


def small_times_wide(small, wide):
    small_high, small_low = halves(small)
    wide_high, wide_low = halves(wide)
    return jnp.dot(
        jnp.concatenate([small_high, small_low, small_high], axis=1),
        jnp.concatenate([wide_high, wide_high, wide_low], axis=0),
        preferred_element_type=F32,
    )


def chained(first, later):
    lane = lax.broadcasted_iota(jnp.int32, first.shape, 1)
    first_high, first_low = halves(first[:, :EMB])
    later_high, later_low = halves(later)
    by_high = jnp.dot(
        jnp.concatenate([first_high, first_low], axis=0), later_high, preferred_element_type=F32
    )
    by_low = jnp.dot(first_high, later_low, preferred_element_type=F32)
    moved = by_high[:EMB] + (by_high[EMB:] + by_low)
    return moved + jnp.where(lane == EMB, first, 0.0)


def packed(value):
    half = EMB // 2
    return jnp.concatenate([value[:half], value[half:]], axis=1)


def unpacked(value):
    return jnp.concatenate([value[:, :MAP], value[:, MAP:]], axis=0)


def chain_of(maps):
    while len(maps) > 1:
        joined = [chained(maps[i], maps[i + 1]) for i in range(0, len(maps) - 1, 2)]
        maps = joined + maps[len(maps) - len(maps) % 2 :]
    return maps[0]


def kernel(
    wide_count,
    narrow_count,
    points_ref,
    start_ref,
    out_ref,
    own_ref,
    near_ref,
    points,
    left_ref,
    right_ref,
    weight_ref,
    weights_ref,
    high_ref,
    low_ref,
    basis_ref,
    image_ref,
    columns_ref,
    stats_ref,
    near_stats_ref,
    send_ref,
    got_ref,
    ring_ref,
    low_maps_ref,
    high_maps_ref,
    next_map_ref,
    load_sem,
    x_send,
    x_recv,
    e_send,
    e_recv,
    s_send,
    s_recv,
    m_send,
    m_recv,
    n_send,
    n_recv,
):
    wide = lax.axis_index("wide")
    narrow = lax.axis_index("narrow")
    total = wide_count * narrow_count
    me = wide * narrow_count + narrow
    after = lax.rem(me + 1, total)
    before = lax.rem(me + total - 1, total)
    after_id = (lax.div(after, narrow_count), lax.rem(after, narrow_count))
    before_id = (lax.div(before, narrow_count), lax.rem(before, narrow_count))
    upper = lax.div(wide, LOW)
    lower = lax.rem(wide, LOW)
    uppers = wide_count // LOW

    def along_narrow(step):
        return (wide, lax.rem(narrow + step, narrow_count))

    def along_lower(step):
        return (upper * LOW + lax.rem(lower + step, LOW), narrow)

    def along_upper(step):
        return (lax.rem(upper + step, uppers) * LOW + lower, narrow)

    levels = (
        (along_narrow, narrow_count, narrow, ring_ref),
        (along_lower, LOW, lower, low_maps_ref),
        (along_upper, uppers, upper, high_maps_ref),
    )
    loads = (
        pltpu.make_async_copy(points_ref, points, load_sem.at[0]),
        pltpu.make_async_copy(start_ref, basis_ref, load_sem.at[1]),
    )
    for copy in loads:
        copy.start()
    barrier = pltpu.get_barrier_semaphore()
    greeted = 0
    for peer in (after_id, before_id):
        pl.semaphore_signal(barrier, inc=1, device_id=peer, device_id_type=MESH)
        greeted += 1
    for peer_at, count, _, _ in levels:
        for step in range(1, count):
            pl.semaphore_signal(barrier, inc=1, device_id=peer_at(step), device_id_type=MESH)
            greeted += 1
    pl.semaphore_wait(barrier, greeted)

    def remote(source, target, send, recv, peer):
        return pltpu.make_async_remote_copy(
            src_ref=source,
            dst_ref=target,
            send_sem=send,
            recv_sem=recv,
            device_id=peer,
            device_id_type=MESH,
        )

    def start_now(copies):
        @pl.when(me >= 0)
        def _():
            for copy in copies:
                copy.start()

    point_copies = []
    done = 0
    for c, size in enumerate(CHUNKS):
        for side, peer in ((0, after_id), (1, before_id)):
            rows = pl.ds(BLOCK - done - size if side == 0 else done, size)
            copy = remote(
                points_ref.at[rows, :],
                near_ref.at[side, rows, :],
                x_send.at[c, side],
                x_recv.at[c, side],
                peer,
            )
            copy.start()
            point_copies.append(copy)
        done += size

    for copy in loads:
        copy.wait()
    origin = jnp.mean(points[...], axis=0, keepdims=True)
    operands = (left_ref, right_ref, weight_ref, weights_ref)
    tile = functools.partial(kernel_tile, *operands, high_ref, low_ref)
    for at in range(0, BLOCK, 256):
        prepare(points[at : at + 256, :] - origin, *operands, BLOCK + at)
    tile(slice(BLOCK, 2 * BLOCK), slice(BLOCK, 2 * BLOCK))
    first, last = BLOCK, 2 * BLOCK
    for c, size in enumerate(CHUNKS):
        for side in (0, 1):
            point_copies[2 * c + side].wait_recv()
            known = slice(first, last)
            added = slice(first - size, first) if side == 0 else slice(last, last + size)
            at = added.start
            here = pl.ds(at - 2 * BLOCK * side, size)
            prepare(near_ref[side, here, :] - origin, *operands, at)
            first, last = min(first, added.start), max(last, added.stop)
            value = tile(slice(first, last), added)
            value = value[known.start - first : known.stop - first].T
            keep(value, high_ref, low_ref, added, known)

    def elimination_and_basis():
        basis = basis_ref[...]
        both = elimination(product_nt(basis, basis))
        basis = basis - jnp.mean(basis, axis=1, keepdims=True)
        pair = jnp.concatenate(halves(basis), axis=0)
        weighted = jnp.sum(basis * weights_ref[...], axis=1, keepdims=True)
        top = jnp.maximum(jnp.max(jnp.abs(basis), axis=1, keepdims=True), 1e-30)
        small = basis * (256.0 / top)
        small_high = small.astype(F8)
        small_low = (small - small_high.astype(F32)).astype(F8)
        small_pair = jnp.concatenate([small_high, small_low], axis=0)
        return both, (pair, small_pair, top / (256.0 * LOW_SCALE), weighted)

    def product(basis, part):
        pair, small_pair, unit, weighted = basis
        cols = slice(part * BLOCK, (part + 1) * BLOCK)
        by_high = jnp.dot(pair, high_ref[:, cols], preferred_element_type=F32)
        by_low = jnp.dot(small_pair, low_ref[:, cols], preferred_element_type=F32)
        by_low = (by_low[:EMB] + by_low[EMB:]) * unit + weighted * weights_ref[:, cols]
        return by_high[:EMB] + (by_high[EMB:] + by_low)

    @pl.loop(0, ITERS - 1)
    def _(_):
        both, basis = elimination_and_basis()
        factor = 0.5 * inverse_factor(eliminated(both, range(EMB - 1)))
        for part in range(3):
            image_ref[:, part * BLOCK : (part + 1) * BLOCK] = product(basis, part)
        image = image_ref[...]
        image = image - jnp.mean(image, axis=1, keepdims=True)
        basis_ref[...] = small_times_wide(factor, image)

    both, basis = elimination_and_basis()
    block_copies = []
    thirds_of_steps = (range(0, 11), range(11, 21), range(21, EMB - 1))
    for steps, part, peer in zip(thirds_of_steps, (1, 2, 0), (after_id, after_id, before_id)):
        both = eliminated(both, steps)
        send_ref[part] = product(basis, part)
        copy = remote(send_ref.at[part], got_ref.at[part], e_send.at[part], e_recv.at[part], peer)
        start_now([copy])
        block_copies.append(copy)
    factor = 0.5 * inverse_factor(both)
    raw = jnp.concatenate([send_ref[0], send_ref[1], send_ref[2]], axis=1)
    raw_mean = jnp.mean(raw, axis=1, keepdims=True)
    image = small_times_wide(factor, raw - raw_mean)
    image = image - jnp.mean(image, axis=1, keepdims=True)
    size = jnp.sum(image * image, axis=1, keepdims=True) + 1e-06
    scale = 1.0 / jnp.sqrt(jnp.sqrt(size))
    to_embedded = jnp.concatenate([factor * scale, jnp.zeros((EMB, MAP - EMB), F32)], axis=1)
    lane = lax.broadcasted_iota(jnp.int32, (EMB, MAP), 1)
    row = lax.broadcasted_iota(jnp.int32, (EMB, MAP), 0)
    stats_ref[...] = packed(jnp.where(lane == EMB, raw_mean, to_embedded))
    for side, peer in ((0, after_id), (1, before_id)):
        copy = remote(
            stats_ref, near_stats_ref.at[side], s_send.at[side], s_recv.at[side], peer
        )
        block_copies.append(copy)
    start_now(block_copies[3:])
    image_ref[:, : 2 * BLOCK] = image[:, : 2 * BLOCK] * scale

    source = image_ref[:, : 2 * BLOCK]
    source_mean = jnp.mean(source, axis=1, keepdims=True)
    source = source - source_mean
    block_copies[0].wait_recv()
    target = got_ref[1]
    covariance = product_nt(target, source[:, :BLOCK])
    target_mean = jnp.sum(target, axis=1, keepdims=True)
    block_copies[1].wait_recv()
    target = got_ref[2]
    covariance = covariance + product_nt(target, source[:, BLOCK:])
    target_mean = (target_mean + jnp.sum(target, axis=1, keepdims=True)) / (2.0 * BLOCK)
    block_copies[3].wait_recv()
    prev_stats = unpacked(near_stats_ref[0])
    prev_mean = prev_stats[:, EMB : EMB + 1]
    covariance = jnp.concatenate([covariance, jnp.zeros((EMB, MAP - EMB), F32)], axis=1)
    covariance = jnp.dot(
        prev_stats[:, :EMB],
        jnp.where(lane == EMB, target_mean - prev_mean, covariance),
        precision=HIGHEST,
        preferred_element_type=F32,
    )
    target_mean = covariance[:, EMB : EMB + 1]
    covariance = covariance[:, :EMB]
    turn = covariance / jnp.sqrt(jnp.sum(covariance * covariance) + 1e-06)

    def newton_schulz(_, turn):
        square = lax.dot_general(
            turn, turn, NT, precision=HIGHEST, preferred_element_type=F32
        )
        return 1.5 * turn - 0.5 * jnp.dot(
            square, turn, precision=HIGHEST, preferred_element_type=F32
        )

    turn = lax.fori_loop(0, NS_STEPS, newton_schulz, turn)
    moved = jnp.dot(
        turn,
        jnp.where(lane == EMB, source_mean, 0.0),
        precision=HIGHEST,
        preferred_element_type=F32,
    )
    own_map = jnp.concatenate([turn, jnp.zeros((EMB, MAP - EMB), F32)], axis=1)
    own_map = own_map + (jnp.where(lane == EMB, target_mean, 0.0) - moved)
    unit = jnp.where(lane == row, 1.0, 0.0)
    has_prev = jnp.where(me > 0, 1.0, 0.0).astype(F32)
    has_next = jnp.where(me < total - 1, 1.0, 0.0).astype(F32)
    share = 1.0 / (1.0 + has_prev + has_next)

    def gather_start(level, value):
        peer_at, count, place, maps_ref = levels[level]
        maps_ref[place] = packed(value)
        copies = []
        for step in range(1, count):
            copy = remote(
                maps_ref.at[place],
                maps_ref.at[place],
                m_send.at[slots[level] + step - 1],
                m_recv.at[slots[level] + step - 1],
                peer_at(step),
            )
            copies.append(copy)
        start_now(copies)
        return copies

    def gather_end(level):
        peer_at, count, place, maps_ref = levels[level]
        for step in range(1, count):
            origin = lax.rem(place + count - step, count)
            remote(
                maps_ref.at[origin],
                maps_ref.at[origin],
                m_send.at[slots[level] + step - 1],
                m_recv.at[slots[level] + step - 1],
                peer_at(step),
            ).wait_recv()
        maps = [unpacked(maps_ref[j]) for j in range(count)]
        masked = []
        for j in range(count - 1):
            earlier = jnp.where(j < place, 1.0, 0.0).astype(F32)
            masked.append(earlier * maps[j] + (1.0 - earlier) * unit)
        return maps, masked

    slots = (0, narrow_count - 1, narrow_count + LOW - 2)
    own_ref[...] = packed(own_map)
    level_copies = gather_start(0, own_map)
    next_copy = remote(own_ref, next_map_ref, n_send, n_recv, before_id)
    start_now([next_copy])
    block_copies[2].wait_recv()
    block_copies[4].wait_recv()
    next_stats = unpacked(near_stats_ref[1])
    columns = jnp.concatenate(
        [
            image_ref[:, BLOCK : 2 * BLOCK],
            small_times_wide(prev_stats[:, :EMB], got_ref[2] - prev_mean),
            small_times_wide(next_stats[:, :EMB], got_ref[0] - next_stats[:, EMB : EMB + 1]),
        ],
        axis=0,
    )
    columns_high, columns_low = halves(columns)
    columns_ref[...] = jnp.concatenate([columns_high, columns_high, columns_low], axis=0)
    maps, masked = gather_end(0)
    level_copies += gather_start(1, chain_of(maps))
    prefix = chain_of(masked)
    next_copy.wait_recv()
    own_and_next = chained(own_map, unpacked(next_map_ref[...]))
    maps, masked = gather_end(1)
    level_copies += gather_start(2, chain_of(maps))
    prefix = chained(chain_of(masked), prefix)
    maps = (
        chained(prefix, own_map) * share,
        prefix * (has_prev * share),
        chained(prefix, own_and_next) * (has_next * share),
    )
    joined_high, joined_low = halves(jnp.concatenate([m[:, :EMB] for m in maps], axis=1))
    aligned = jnp.dot(
        jnp.concatenate([joined_high, joined_low, joined_high], axis=1),
        columns_ref[...],
        preferred_element_type=F32,
    )
    aligned = aligned + (maps[0] + maps[1] + maps[2])[:, EMB : EMB + 1]
    _, masked = gather_end(2)
    outer = chain_of(masked)
    out_ref[...] = small_times_wide(outer[:, :EMB], aligned) + outer[:, EMB : EMB + 1]
    for copy in point_copies + block_copies + level_copies + [next_copy]:
        copy.wait_send()


def shards(wide_count, narrow_count, points, start_basis):
    messages = (narrow_count - 1) + (LOW - 1) + (wide_count // LOW - 1)
    in_vmem = pl.BlockSpec(memory_space=pltpu.VMEM)
    return pl.pallas_call(
        functools.partial(kernel, wide_count, narrow_count),
        out_shape=jax.ShapeDtypeStruct((EMB, BLOCK), F32),
        in_specs=[pl.BlockSpec(memory_space=pl.ANY)] * 2,
        out_specs=in_vmem,
        scratch_shapes=[
            pltpu.VMEM((EMB // 2, 2 * MAP), F32),
            pltpu.VMEM((2, BLOCK, DIM), F32),
            pltpu.VMEM((BLOCK, DIM), F32),
            pltpu.VMEM((PATCH, 4 * DIM), BF16),
            pltpu.VMEM((4 * DIM, PATCH), BF16),
            pltpu.VMEM((PATCH, 128), F32),
            pltpu.VMEM((1, PATCH), F32),
            pltpu.VMEM((PATCH, PATCH), BF16),
            pltpu.VMEM((PATCH, PATCH), F8),
            pltpu.VMEM((EMB, PATCH), F32),
            pltpu.VMEM((EMB, PATCH), F32),
            pltpu.VMEM((9 * EMB, BLOCK), BF16),
            pltpu.VMEM((EMB // 2, 2 * MAP), F32),
            pltpu.VMEM((2, EMB // 2, 2 * MAP), F32),
            pltpu.VMEM((3, EMB, BLOCK), F32),
            pltpu.VMEM((3, EMB, BLOCK), F32),
            pltpu.VMEM((narrow_count, EMB // 2, 2 * MAP), F32),
            pltpu.VMEM((LOW, EMB // 2, 2 * MAP), F32),
            pltpu.VMEM((wide_count // LOW, EMB // 2, 2 * MAP), F32),
            pltpu.VMEM((EMB // 2, 2 * MAP), F32),
            pltpu.SemaphoreType.DMA((2,)),
            pltpu.SemaphoreType.DMA((len(CHUNKS), 2)),
            pltpu.SemaphoreType.DMA((len(CHUNKS), 2)),
            pltpu.SemaphoreType.DMA((3,)),
            pltpu.SemaphoreType.DMA((3,)),
            pltpu.SemaphoreType.DMA((2,)),
            pltpu.SemaphoreType.DMA((2,)),
            pltpu.SemaphoreType.DMA((messages,)),
            pltpu.SemaphoreType.DMA((messages,)),
            pltpu.SemaphoreType.DMA,
            pltpu.SemaphoreType.DMA,
        ],
        compiler_params=pltpu.CompilerParams(
            collective_id=0, has_side_effects=True, vmem_limit_bytes=61 * 1024 * 1024
        ),
    )(points, start_basis)


def solution(mesh):
    placed = (P(("wide", "narrow"), None), P(None, ("wide", "narrow")))
    return jax.shard_map(
        functools.partial(shards, mesh.shape["wide"], mesh.shape["narrow"]),
        mesh=mesh,
        in_specs=placed,
        out_specs=P(None, ("wide", "narrow")),
        check_vma=False,
    )
```

```python
import functools
import math

import jax
import jax.numpy as jnp
from jax import lax
from jax.experimental import pallas as pl
from jax.experimental.pallas import tpu as pltpu
from jax.sharding import PartitionSpec as P

DIM = 128
EMB = 32
BLOCK = 1024
PATCH = 3 * BLOCK
ITERS = 4
NS_STEPS = 16
CHUNKS = (256, 256, 256, 256)
MAP = 64
LOW = 8

F32 = jnp.float32
BF16 = jnp.bfloat16
F8 = jnp.float8_e4m3fn
LOW_SCALE = 65536.0
F8_MAX = 448.0
NT = (((1,), (1,)), ((), ()))
HIGHEST = lax.Precision.HIGHEST
MESH = pl.DeviceIdType.MESH
SCALE = math.sqrt(2.0 * math.log2(math.e) / (0.5 * DIM))


def halves(value):
    high = value.astype(BF16)
    return high, (value - high.astype(F32)).astype(BF16)


def thirds(value):
    high = value.astype(BF16)
    rest = value - high.astype(F32)
    middle = rest.astype(BF16)
    return high, middle, (rest - middle.astype(F32)).astype(BF16)


def prepare(rows, left_ref, right_ref, weight_ref, weights_ref, at):
    count = rows.shape[0]
    scaled = rows * SCALE
    high, low = halves(scaled)
    norms = -0.5 * jnp.sum(scaled * scaled, axis=1, keepdims=True)
    n0, n1, n2 = (part.astype(F32) for part in thirds(norms))
    lane = lax.broadcasted_iota(jnp.int32, (count, DIM), 1)
    tail = jnp.where(
        lane == 0,
        n0,
        jnp.where(lane == 1, n1, jnp.where(lane == 2, n2, jnp.where(lane < 6, 1.0, 0.0))),
    )
    here = pl.ds(at, count)
    left_ref[here, 0:DIM] = high
    left_ref[here, DIM : 2 * DIM] = low
    left_ref[here, 2 * DIM : 3 * DIM] = high
    left_ref[here, 3 * DIM : 4 * DIM] = tail.astype(BF16)
    weight_ref[here, :] = jnp.broadcast_to(jnp.exp2(norms), (count, 128))
    turned = scaled.T
    high, low = halves(turned)
    norms = -0.5 * jnp.sum(turned * turned, axis=0, keepdims=True)
    n0, n1, n2 = (part.astype(F32) for part in thirds(norms))
    row = lax.broadcasted_iota(jnp.int32, (DIM, count), 0)
    tail = jnp.where(
        row < 3,
        1.0,
        jnp.where(row == 3, n0, jnp.where(row == 4, n1, jnp.where(row == 5, n2, 0.0))),
    )
    right_ref[0:DIM, here] = high
    right_ref[DIM : 2 * DIM, here] = high
    right_ref[2 * DIM : 3 * DIM, here] = low
    right_ref[3 * DIM : 4 * DIM, here] = tail.astype(BF16)
    weights_ref[:, here] = jnp.exp2(norms)


def kernel_tile(left_ref, right_ref, weight_ref, weights_ref, high_ref, low_ref, rows, cols):
    power = jnp.dot(left_ref[rows, :], right_ref[:, cols], preferred_element_type=F32)
    repeats = (cols.stop - cols.start) // 128
    value = jnp.exp2(power) - jnp.tile(weight_ref[rows, :], (1, repeats)) * weights_ref[:, cols]
    keep(value, high_ref, low_ref, rows, cols)
    return value


def keep(value, high_ref, low_ref, rows, cols):
    high = value.astype(BF16)
    rest = (value - high.astype(F32)) * LOW_SCALE
    high_ref[rows, cols] = high
    low_ref[rows, cols] = jnp.minimum(jnp.maximum(rest, -F8_MAX), F8_MAX).astype(F8)


def product_nt(a, b):
    rows = a.shape[0]
    pair_a = jnp.concatenate(halves(a), axis=0)
    pair_b = jnp.concatenate(halves(b), axis=0)
    full = lax.dot_general(pair_a, pair_b, NT, preferred_element_type=F32)
    return full[:rows, :rows] + (full[:rows, rows:] + full[rows:, :rows]) + full[rows:, rows:]


def elimination(gram):
    n = gram.shape[0]
    lane = lax.broadcasted_iota(jnp.int32, (n, 128), 1)
    row = lax.broadcasted_iota(jnp.int32, (n, 128), 0)
    both = jnp.concatenate([gram, jnp.zeros((n, 128 - n), F32)], axis=1)
    return jnp.where(lane == row + n, 1.0, both)


def eliminated(both, columns):
    row = lax.broadcasted_iota(jnp.int32, both.shape, 0)
    for k in columns:
        pivot = both[k : k + 1, :] / both[k : k + 1, k : k + 1]
        both = jnp.where(row > k, both - both[:, k : k + 1] * pivot, both)
    return both


def inverse_factor(both):
    n = both.shape[0]
    lane = lax.broadcasted_iota(jnp.int32, both.shape, 1)
    row = lax.broadcasted_iota(jnp.int32, both.shape, 0)
    diagonal = jnp.sum(jnp.where(lane == row, both, 0.0), axis=1, keepdims=True)
    return both[:, n : 2 * n] / jnp.sqrt(diagonal)


def small_times_wide(small, wide):
    small_high, small_low = halves(small)
    wide_high, wide_low = halves(wide)
    return jnp.dot(
        jnp.concatenate([small_high, small_low, small_high], axis=1),
        jnp.concatenate([wide_high, wide_high, wide_low], axis=0),
        preferred_element_type=F32,
    )


def chained(first, later):
    lane = lax.broadcasted_iota(jnp.int32, first.shape, 1)
    first_high, first_low = halves(first[:, :EMB])
    later_high, later_low = halves(later)
    by_high = jnp.dot(
        jnp.concatenate([first_high, first_low], axis=0), later_high, preferred_element_type=F32
    )
    by_low = jnp.dot(first_high, later_low, preferred_element_type=F32)
    moved = by_high[:EMB] + (by_high[EMB:] + by_low)
    return moved + jnp.where(lane == EMB, first, 0.0)


def packed(value):
    half = EMB // 2
    return jnp.concatenate([value[:half], value[half:]], axis=1)


def unpacked(value):
    return jnp.concatenate([value[:, :MAP], value[:, MAP:]], axis=0)


def chain_of(maps):
    while len(maps) > 1:
        joined = [chained(maps[i], maps[i + 1]) for i in range(0, len(maps) - 1, 2)]
        maps = joined + maps[len(maps) - len(maps) % 2 :]
    return maps[0]


def kernel(
    wide_count,
    narrow_count,
    points_ref,
    start_ref,
    out_ref,
    own_ref,
    near_ref,
    points,
    left_ref,
    right_ref,
    weight_ref,
    weights_ref,
    high_ref,
    low_ref,
    basis_ref,
    image_ref,
    columns_ref,
    stats_ref,
    near_stats_ref,
    send_ref,
    got_ref,
    ring_ref,
    low_maps_ref,
    high_maps_ref,
    next_map_ref,
    load_sem,
    x_send,
    x_recv,
    e_send,
    e_recv,
    s_send,
    s_recv,
    m_send,
    m_recv,
    n_send,
    n_recv,
):
    wide = lax.axis_index("wide")
    narrow = lax.axis_index("narrow")
    total = wide_count * narrow_count
    me = wide * narrow_count + narrow
    after = lax.rem(me + 1, total)
    before = lax.rem(me + total - 1, total)
    after_id = (lax.div(after, narrow_count), lax.rem(after, narrow_count))
    before_id = (lax.div(before, narrow_count), lax.rem(before, narrow_count))
    upper = lax.div(wide, LOW)
    lower = lax.rem(wide, LOW)
    uppers = wide_count // LOW

    def along_narrow(step):
        return (wide, lax.rem(narrow + step, narrow_count))

    def along_lower(step):
        return (upper * LOW + lax.rem(lower + step, LOW), narrow)

    def along_upper(step):
        return (lax.rem(upper + step, uppers) * LOW + lower, narrow)

    levels = (
        (along_narrow, narrow_count, narrow, ring_ref),
        (along_lower, LOW, lower, low_maps_ref),
        (along_upper, uppers, upper, high_maps_ref),
    )
    loads = (
        pltpu.make_async_copy(points_ref, points, load_sem.at[0]),
        pltpu.make_async_copy(start_ref, basis_ref, load_sem.at[1]),
    )
    for copy in loads:
        copy.start()
    barrier = pltpu.get_barrier_semaphore()
    greeted = 0
    for peer in (after_id, before_id):
        pl.semaphore_signal(barrier, inc=1, device_id=peer, device_id_type=MESH)
        greeted += 1
    for peer_at, count, _, _ in levels:
        for step in range(1, count):
            pl.semaphore_signal(barrier, inc=1, device_id=peer_at(step), device_id_type=MESH)
            greeted += 1
    pl.semaphore_wait(barrier, greeted)

    def remote(source, target, send, recv, peer):
        return pltpu.make_async_remote_copy(
            src_ref=source,
            dst_ref=target,
            send_sem=send,
            recv_sem=recv,
            device_id=peer,
            device_id_type=MESH,
        )

    def start_now(copies):
        @pl.when(me >= 0)
        def _():
            for copy in copies:
                copy.start()

    point_copies = []
    done = 0
    for c, size in enumerate(CHUNKS):
        for side, peer in ((0, after_id), (1, before_id)):
            rows = pl.ds(BLOCK - done - size if side == 0 else done, size)
            copy = remote(
                points_ref.at[rows, :],
                near_ref.at[side, rows, :],
                x_send.at[c, side],
                x_recv.at[c, side],
                peer,
            )
            copy.start()
            point_copies.append(copy)
        done += size

    for copy in loads:
        copy.wait()
    origin = jnp.mean(points[...], axis=0, keepdims=True)
    operands = (left_ref, right_ref, weight_ref, weights_ref)
    tile = functools.partial(kernel_tile, *operands, high_ref, low_ref)
    for at in range(0, BLOCK, 256):
        prepare(points[at : at + 256, :] - origin, *operands, BLOCK + at)
    tile(slice(BLOCK, 2 * BLOCK), slice(BLOCK, 2 * BLOCK))
    first, last = BLOCK, 2 * BLOCK
    for c, size in enumerate(CHUNKS):
        known, grown = slice(first, last), slice(first - size, last + size)
        sides = (slice(first - size, first), slice(last, last + size))
        for side in (0, 1):
            point_copies[2 * c + side].wait_recv()
            at = sides[side].start
            here = pl.ds(at - 2 * BLOCK * side, size)
            prepare(near_ref[side, here, :] - origin, *operands, at)
        for side in (0, 1):
            value = tile(grown, sides[side])[size : size + last - first].T
            keep(value, high_ref, low_ref, sides[side], known)
        first, last = grown.start, grown.stop

    def elimination_and_basis():
        basis = basis_ref[...]
        both = elimination(product_nt(basis, basis))
        basis = basis - jnp.mean(basis, axis=1, keepdims=True)
        pair = jnp.concatenate(halves(basis), axis=0)
        weighted = jnp.sum(basis * weights_ref[...], axis=1, keepdims=True)
        top = jnp.maximum(jnp.max(jnp.abs(basis), axis=1, keepdims=True), 1e-30)
        small = basis * (256.0 / top)
        small_high = small.astype(F8)
        small_low = (small - small_high.astype(F32)).astype(F8)
        small_pair = jnp.concatenate([small_high, small_low], axis=0)
        return both, (pair, small_pair, top / (256.0 * LOW_SCALE), weighted)

    def product(basis, part):
        pair, small_pair, unit, weighted = basis
        cols = slice(part * BLOCK, (part + 1) * BLOCK)
        by_high = jnp.dot(pair, high_ref[:, cols], preferred_element_type=F32)
        by_low = jnp.dot(small_pair, low_ref[:, cols], preferred_element_type=F32)
        by_low = (by_low[:EMB] + by_low[EMB:]) * unit + weighted * weights_ref[:, cols]
        return by_high[:EMB] + (by_high[EMB:] + by_low)

    @pl.loop(0, ITERS - 1)
    def _(_):
        both, basis = elimination_and_basis()
        factor = 0.5 * inverse_factor(eliminated(both, range(EMB - 1)))
        for part in range(3):
            image_ref[:, part * BLOCK : (part + 1) * BLOCK] = product(basis, part)
        image = image_ref[...]
        image = image - jnp.mean(image, axis=1, keepdims=True)
        basis_ref[...] = small_times_wide(factor, image)

    both, basis = elimination_and_basis()
    block_copies = []
    thirds_of_steps = (range(0, 11), range(11, 21), range(21, EMB - 1))
    for steps, part, peer in zip(thirds_of_steps, (1, 2, 0), (after_id, after_id, before_id)):
        both = eliminated(both, steps)
        send_ref[part] = product(basis, part)
        copy = remote(send_ref.at[part], got_ref.at[part], e_send.at[part], e_recv.at[part], peer)
        start_now([copy])
        block_copies.append(copy)
    factor = 0.5 * inverse_factor(both)
    raw = jnp.concatenate([send_ref[0], send_ref[1], send_ref[2]], axis=1)
    raw_mean = jnp.mean(raw, axis=1, keepdims=True)
    image = small_times_wide(factor, raw - raw_mean)
    image = image - jnp.mean(image, axis=1, keepdims=True)
    size = jnp.sum(image * image, axis=1, keepdims=True) + 1e-06
    scale = 1.0 / jnp.sqrt(jnp.sqrt(size))
    to_embedded = jnp.concatenate([factor * scale, jnp.zeros((EMB, MAP - EMB), F32)], axis=1)
    lane = lax.broadcasted_iota(jnp.int32, (EMB, MAP), 1)
    row = lax.broadcasted_iota(jnp.int32, (EMB, MAP), 0)
    stats_ref[...] = packed(jnp.where(lane == EMB, raw_mean, to_embedded))
    for side, peer in ((0, after_id), (1, before_id)):
        copy = remote(
            stats_ref, near_stats_ref.at[side], s_send.at[side], s_recv.at[side], peer
        )
        block_copies.append(copy)
    start_now(block_copies[3:])
    image_ref[:, : 2 * BLOCK] = image[:, : 2 * BLOCK] * scale

    source = image_ref[:, : 2 * BLOCK]
    source_mean = jnp.mean(source, axis=1, keepdims=True)
    source = source - source_mean
    block_copies[0].wait_recv()
    target = got_ref[1]
    covariance = product_nt(target, source[:, :BLOCK])
    target_mean = jnp.sum(target, axis=1, keepdims=True)
    block_copies[1].wait_recv()
    target = got_ref[2]
    covariance = covariance + product_nt(target, source[:, BLOCK:])
    target_mean = (target_mean + jnp.sum(target, axis=1, keepdims=True)) / (2.0 * BLOCK)
    block_copies[3].wait_recv()
    prev_stats = unpacked(near_stats_ref[0])
    prev_mean = prev_stats[:, EMB : EMB + 1]
    covariance = jnp.concatenate([covariance, jnp.zeros((EMB, MAP - EMB), F32)], axis=1)
    covariance = jnp.dot(
        prev_stats[:, :EMB],
        jnp.where(lane == EMB, target_mean - prev_mean, covariance),
        precision=HIGHEST,
        preferred_element_type=F32,
    )
    target_mean = covariance[:, EMB : EMB + 1]
    covariance = covariance[:, :EMB]
    turn = covariance / jnp.sqrt(jnp.sum(covariance * covariance) + 1e-06)

    def newton_schulz(_, turn):
        square = lax.dot_general(
            turn, turn, NT, precision=HIGHEST, preferred_element_type=F32
        )
        return 1.5 * turn - 0.5 * jnp.dot(
            square, turn, precision=HIGHEST, preferred_element_type=F32
        )

    turn = lax.fori_loop(0, NS_STEPS, newton_schulz, turn)
    moved = jnp.dot(
        turn,
        jnp.where(lane == EMB, source_mean, 0.0),
        precision=HIGHEST,
        preferred_element_type=F32,
    )
    own_map = jnp.concatenate([turn, jnp.zeros((EMB, MAP - EMB), F32)], axis=1)
    own_map = own_map + (jnp.where(lane == EMB, target_mean, 0.0) - moved)
    unit = jnp.where(lane == row, 1.0, 0.0)
    has_prev = jnp.where(me > 0, 1.0, 0.0).astype(F32)
    has_next = jnp.where(me < total - 1, 1.0, 0.0).astype(F32)
    share = 1.0 / (1.0 + has_prev + has_next)

    def gather_start(level, value):
        peer_at, count, place, maps_ref = levels[level]
        maps_ref[place] = packed(value)
        copies = []
        for step in range(1, count):
            copy = remote(
                maps_ref.at[place],
                maps_ref.at[place],
                m_send.at[slots[level] + step - 1],
                m_recv.at[slots[level] + step - 1],
                peer_at(step),
            )
            copies.append(copy)
        start_now(copies)
        return copies

    def gather_end(level):
        peer_at, count, place, maps_ref = levels[level]
        for step in range(1, count):
            origin = lax.rem(place + count - step, count)
            remote(
                maps_ref.at[origin],
                maps_ref.at[origin],
                m_send.at[slots[level] + step - 1],
                m_recv.at[slots[level] + step - 1],
                peer_at(step),
            ).wait_recv()
        maps = [unpacked(maps_ref[j]) for j in range(count)]
        masked = []
        for j in range(count - 1):
            earlier = jnp.where(j < place, 1.0, 0.0).astype(F32)
            masked.append(earlier * maps[j] + (1.0 - earlier) * unit)
        return maps, masked

    slots = (0, narrow_count - 1, narrow_count + LOW - 2)
    own_ref[...] = packed(own_map)
    level_copies = gather_start(0, own_map)
    next_copy = remote(own_ref, next_map_ref, n_send, n_recv, before_id)
    start_now([next_copy])
    block_copies[2].wait_recv()
    block_copies[4].wait_recv()
    next_stats = unpacked(near_stats_ref[1])
    columns = jnp.concatenate(
        [
            image_ref[:, BLOCK : 2 * BLOCK],
            small_times_wide(prev_stats[:, :EMB], got_ref[2] - prev_mean),
            small_times_wide(next_stats[:, :EMB], got_ref[0] - next_stats[:, EMB : EMB + 1]),
        ],
        axis=0,
    )
    columns_high, columns_low = halves(columns)
    columns_ref[...] = jnp.concatenate([columns_high, columns_high, columns_low], axis=0)
    maps, masked = gather_end(0)
    level_copies += gather_start(1, chain_of(maps))
    prefix = chain_of(masked)
    next_copy.wait_recv()
    own_and_next = chained(own_map, unpacked(next_map_ref[...]))
    maps, masked = gather_end(1)
    level_copies += gather_start(2, chain_of(maps))
    prefix = chained(chain_of(masked), prefix)
    maps = (
        chained(prefix, own_map) * share,
        prefix * (has_prev * share),
        chained(prefix, own_and_next) * (has_next * share),
    )
    joined_high, joined_low = halves(jnp.concatenate([m[:, :EMB] for m in maps], axis=1))
    aligned = jnp.dot(
        jnp.concatenate([joined_high, joined_low, joined_high], axis=1),
        columns_ref[...],
        preferred_element_type=F32,
    )
    aligned = aligned + (maps[0] + maps[1] + maps[2])[:, EMB : EMB + 1]
    _, masked = gather_end(2)
    outer = chain_of(masked)
    out_ref[...] = small_times_wide(outer[:, :EMB], aligned) + outer[:, EMB : EMB + 1]
    for copy in point_copies + block_copies + level_copies + [next_copy]:
        copy.wait_send()


def shards(wide_count, narrow_count, points, start_basis):
    messages = (narrow_count - 1) + (LOW - 1) + (wide_count // LOW - 1)
    in_vmem = pl.BlockSpec(memory_space=pltpu.VMEM)
    return pl.pallas_call(
        functools.partial(kernel, wide_count, narrow_count),
        out_shape=jax.ShapeDtypeStruct((EMB, BLOCK), F32),
        in_specs=[pl.BlockSpec(memory_space=pl.ANY)] * 2,
        out_specs=in_vmem,
        scratch_shapes=[
            pltpu.VMEM((EMB // 2, 2 * MAP), F32),
            pltpu.VMEM((2, BLOCK, DIM), F32),
            pltpu.VMEM((BLOCK, DIM), F32),
            pltpu.VMEM((PATCH, 4 * DIM), BF16),
            pltpu.VMEM((4 * DIM, PATCH), BF16),
            pltpu.VMEM((PATCH, 128), F32),
            pltpu.VMEM((1, PATCH), F32),
            pltpu.VMEM((PATCH, PATCH), BF16),
            pltpu.VMEM((PATCH, PATCH), F8),
            pltpu.VMEM((EMB, PATCH), F32),
            pltpu.VMEM((EMB, PATCH), F32),
            pltpu.VMEM((9 * EMB, BLOCK), BF16),
            pltpu.VMEM((EMB // 2, 2 * MAP), F32),
            pltpu.VMEM((2, EMB // 2, 2 * MAP), F32),
            pltpu.VMEM((3, EMB, BLOCK), F32),
            pltpu.VMEM((3, EMB, BLOCK), F32),
            pltpu.VMEM((narrow_count, EMB // 2, 2 * MAP), F32),
            pltpu.VMEM((LOW, EMB // 2, 2 * MAP), F32),
            pltpu.VMEM((wide_count // LOW, EMB // 2, 2 * MAP), F32),
            pltpu.VMEM((EMB // 2, 2 * MAP), F32),
            pltpu.SemaphoreType.DMA((2,)),
            pltpu.SemaphoreType.DMA((len(CHUNKS), 2)),
            pltpu.SemaphoreType.DMA((len(CHUNKS), 2)),
            pltpu.SemaphoreType.DMA((3,)),
            pltpu.SemaphoreType.DMA((3,)),
            pltpu.SemaphoreType.DMA((2,)),
            pltpu.SemaphoreType.DMA((2,)),
            pltpu.SemaphoreType.DMA((messages,)),
            pltpu.SemaphoreType.DMA((messages,)),
            pltpu.SemaphoreType.DMA,
            pltpu.SemaphoreType.DMA,
        ],
        compiler_params=pltpu.CompilerParams(
            collective_id=0, has_side_effects=True, vmem_limit_bytes=61 * 1024 * 1024
        ),
    )(points, start_basis)


def solution(mesh):
    placed = (P(("wide", "narrow"), None), P(None, ("wide", "narrow")))
    return jax.shard_map(
        functools.partial(shards, mesh.shape["wide"], mesh.shape["narrow"]),
        mesh=mesh,
        in_specs=placed,
        out_specs=P(None, ("wide", "narrow")),
        check_vma=False,
    )
```
